256 devices in a mesh: lon: 16 (over x_hi, y, core), lat: 8 (over z), comp: 2 (over x_lo).
Axes of the slice: x: 4 (x_hi: 2, x_lo: 2; x = x_hi * 2 + x_lo), y: 4, z: 8, core: 2. Of those that a mesh axis runs over, the one named last changes fastest.
Arguments:
- state: float32 [2, 2, 64, 128, 4096], P('comp', None, None, 'lat', 'lon'), may hold values from -6 to 6
- params: float32 [2, 3, 2, 128, 4096], P('comp', None, None, 'lat', 'lon'), may hold values from -2 to 10, as said below
- couple_weight: float32 [2, 8, 2, 64], P('comp'), may hold values from -0.5 to 0.5
- weight_table: float32 [2, 4, 2], P('comp'), may hold values from 0.2 to 0.8
- intersection_map: int32 [2, 128, 4096], P('comp', 'lat', 'lon'), may hold values from 0 to 15
- sea_mask: int32 [2, 128, 4096], P('comp', 'lat', 'lon'), may hold values 0 or 1
Outputs:
- new_state: float32 [2, 2, 64, 128, 4096], P('comp', None, None, 'lat', 'lon')
- coupled: float32 [2, 8, 128, 4096], P('comp', None, 'lat', 'lon')
The draws below stay inside these ranges and needn't reach their ends.
Inputs may be any that keep to these rules, and one draw needn't show every extreme that they name: `params`: along dimension 1: horizontal diffusion numbers from 0.03 to 0.24, vertical diffusion numbers from 0.1 to 10, surface forcing from -2 to 2.
All inputs are finite; a program needn't handle non-finite values. No bound on the sum of `sea_mask` on one device may be relied on, other than what follows from the above.
Results may differ from the reference program's by a relative error of at most 0.0001.
Values sent between devices are 32-bit elements; how exact they have to be, the bound alone decides.
No kernel may reach another device: no remote copies, remote signals or barrier semaphores. Data moves between devices by JAX's collectives and lax.ppermute only.
A program may use at most 128 MiB of HBM per device.

```python
import jax
import jax.numpy as jnp
from jax import lax

LEV = 64
STEPS = 4
NQ = 8
NW = 4
NY = 128
NX = 4096


def draw_params(key, part):
    key = jax.random.fold_in(key, 11)
    first_key, second_key, third_key = jax.random.split(key, 3)
    shape = (2, 2, NY, NX)
    horizontal = jnp.exp(jax.random.uniform(first_key, shape, jnp.float32, jnp.log(0.03), jnp.log(0.24)))
    vertical = jnp.exp(jax.random.uniform(second_key, shape, jnp.float32, jnp.log(0.1), jnp.log(10.0)))
    forcing = jnp.clip(0.5 * jax.random.normal(third_key, shape, jnp.float32), -2.0, 2.0)
    return jnp.stack([horizontal, vertical, forcing], axis=1).astype(jnp.float32)


def plant(drawn, rng, smallest, top_value):
    shape = drawn.shape
    spot = [jax.random.randint(jax.random.fold_in(rng, axis), (), 0, shape[axis]) for axis in range(len(shape))]
    drawn = drawn.at[tuple(spot)].set(smallest)
    longest = shape.index(max(shape))
    spot[longest] = (spot[longest] + 1) % shape[longest]
    return drawn.at[tuple(spot)].set(top_value)


def block_levels(key, dims, cuts, low, largest):
    def one(position, blocks):
        draws = jax.random.uniform(jax.random.fold_in(jax.random.fold_in(key, 6), position), (blocks,), jnp.float32, low / len(cuts), largest / len(cuts))
        return jnp.repeat(jnp.exp(draws), dims[position] // blocks).reshape((-1,) + (1,) * (len(dims) - position - 1))

    factor_of = one(*cuts[0])
    for cut in cuts[1:]:
        factor_of = factor_of * one(*cut)
    return factor_of


def gaussian(key, shape, width, bound, pieces=(), dtype=jnp.bfloat16):
    array = width * jax.random.normal(key, shape, jnp.float32)
    if pieces:
        array = array * block_levels(key, shape, pieces, -0.22, 0.18)
    return jnp.clip(array, -bound, bound).astype(dtype)


def setup_inputs(seed: int = 0) -> dict:
    key_of = jax.random.split(jax.random.key(seed), 7)
    return {
        "state": gaussian(key_of[0], (2, 2, LEV, NY, NX), 1.0, 6.0, ((0, 2), (3, 8), (4, 16)), jnp.float32),
        "params": draw_params(jax.random.fold_in(key_of[6], 71), 0),
        "couple_weight": gaussian(key_of[2], (2, NQ, 2, LEV), (2 * LEV) ** -0.5, 0.5, ((0, 2),), jnp.float32),
        "weight_table": jnp.clip(0.2 + 0.6 * jax.random.uniform(key_of[3], (2, NW, 2), jnp.float32) ** block_levels(key_of[3], (2, NW, 2), ((0, 2),), -0.2, 0.2), 0.2, 0.8),
        "intersection_map": plant(jax.random.randint(key_of[4], (2, NY, NX), 0, 4 * NW), jax.random.fold_in(key_of[4], 1), 0, (4 * NW) - 1).astype(jnp.int32),
        "sea_mask": plant((jax.random.randint(key_of[5], (2, NY, NX), 0, 10) < 7).astype(jnp.int32), jax.random.fold_in(key_of[5], 1), 0, 1),
    }


def column_solve(right_side, mixing):
    levels = right_side.shape[1]
    pivot_inv = 1.0 / (1.0 + mixing)
    upper_list = [-mixing * pivot_inv]
    carried_list = [right_side[:, 0] * pivot_inv]
    for level_idx in range(1, levels):
        if level_idx < levels - 1:
            diagonal = 1.0 + 2.0 * mixing
        else:
            diagonal = 1.0 + mixing
        pivot_inv = 1.0 / (diagonal + mixing * upper_list[-1])
        upper_list.append(-mixing * pivot_inv)
        carried_list.append((right_side[:, level_idx] + mixing * carried_list[-1]) * pivot_inv)
    solved = carried_list[-1]
    outputs = [solved]
    for level_idx in range(levels - 2, -1, -1):
        solved = carried_list[level_idx] - upper_list[level_idx] * solved
        outputs.append(solved)
    return jnp.stack(outputs[::-1], axis=1)


def advance(padded, column_params):
    centre = padded[:, :, 1:-1, 1:-1]
    laplace_term = (padded[:, :, 2:, 1:-1] + padded[:, :, :-2, 1:-1] + padded[:, :, 1:-1, 2:]
                    + padded[:, :, 1:-1, :-2] - 4.0 * centre)
    right_side = centre + column_params[0][:, None] * laplace_term
    right_side = right_side.at[:, 0].add(column_params[2])
    return column_solve(right_side, column_params[1])


def surface_package(current, weights):
    fields, levels, rows, cols = current.shape
    flat = current.reshape(fields * levels, rows * cols)
    mixed = jnp.dot(weights.reshape(weights.shape[0], fields * levels), flat,
                    precision=lax.Precision.HIGHEST, preferred_element_type=jnp.float32)
    return jnp.tanh(mixed).reshape(weights.shape[0], rows, cols)


def run_section(inputs):
    current, column_params, weights = inputs
    summed = jnp.zeros((weights.shape[0],) + current.shape[2:], jnp.float32)
    for segment_index in range(STEPS):
        padded = jnp.pad(current, ((0, 0), (0, 0), (0, 0), (1, 1)), mode="wrap")
        padded = jnp.pad(padded, ((0, 0), (0, 0), (1, 1), (0, 0)))
        current = advance(padded, column_params)
        summed = summed + surface_package(current, weights)
    return current, summed / STEPS


def remap_onto(sent, table, intersection_code, sea):
    offset = intersection_code % 4
    weight_row = intersection_code // 4
    first = table[:, 0][weight_row]
    second = table[:, 1][weight_row]
    result = jnp.zeros_like(sent)
    for shift_idx in range(4):
        near = jnp.roll(sent, 2 - shift_idx, axis=-1)
        beyond = jnp.roll(sent, 1 - shift_idx, axis=-1)
        candidate = first * near + second * beyond
        result = jnp.where(offset == shift_idx, candidate, result)
    return jnp.where(sea == 1, result, 0.0)


def reference(state, params, couple_weight, weight_table, intersection_map, sea_mask):
    new_state, means = lax.map(run_section, (state, params, couple_weight))
    coupled = jnp.stack([
        remap_onto(means[1], weight_table[0], intersection_map[0], sea_mask[0]),
        remap_onto(means[0], weight_table[1], intersection_map[1], sea_mask[1]),
    ], axis=0)
    return new_state, coupled
```

```python
import jax
import jax.numpy as jnp
from jax import lax
from jax.experimental import pallas as pl
from jax.experimental.pallas import tpu as pltpu
from jax.sharding import PartitionSpec as P

STEPS = 4
LEV = 64
HALF = LEV // 2
ROWS = 16
HALO = 4
COLS = 256
NQ = 8
PAD = 8
TALL = ROWS + 2 * HALO + 2 * PAD
TILES = (ROWS + 2 * HALO) // 8
PLANES = LEV + 3
STRIPS = HALF // 2 + 2
FLAT = HALF * (ROWS + 2 * HALO)
VMEM = pl.BlockSpec(memory_space=pltpu.VMEM)
SMEM = pl.BlockSpec(memory_space=pltpu.SMEM)
F32 = jnp.float32


def lanes():
    return lax.broadcasted_iota(jnp.int32, (8, 128), 1)


def roll(value, shift):
    return pltpu.roll(value, shift % 128, 1)


def pack_kernel(state, params, low_rows, high_rows, strips):
    lane = lanes()

    def rim_rows(i, carry):
        for u in range(4):
            lev = i * 4 + u
            for f in range(2):
                low_rows[f, lev] = state[0, f, lev, 0:HALO]
                high_rows[f, lev] = state[0, f, lev, ROWS - HALO:ROWS]
        return carry

    lax.fori_loop(0, LEV // 4, rim_rows, 0)
    for f in range(2):
        for kind in range(3):
            low_rows[f, LEV + kind] = params[0, kind, f, 0:HALO]
            high_rows[f, LEV + kind] = params[0, kind, f, ROWS - HALO:ROWS]

    def place(total, source, index):
        ring = jnp.where(lane >= 124, source[1], source[0])
        first = roll(ring, 16 * index + 4)
        second = roll(ring, 16 * index + 12)
        inside = (lane >= 16 * index) & (lane < 16 * index + 16)
        pair = jnp.where((lane & 8) == 0, first, second)
        return pair if total is None else jnp.where(inside, pair, total)

    def strip(block, carry):
        for rt in range(2):
            rows = slice(8 * rt, 8 * rt + 8)
            total = None
            for lq in range(2):
                level = block * 2 + lq
                for f in range(2):
                    for h in range(2):
                        lam = level if h == 0 else LEV - 1 - level
                        source = [state[0, f, lam, rows, 128 * c:128 * c + 128] for c in range(2)]
                        total = place(total, source, lq * 4 + f * 2 + h)
            strips[block, rows] = total
        return carry

    lax.fori_loop(0, HALF // 2, strip, 0)
    for rt in range(2):
        rows = slice(8 * rt, 8 * rt + 8)
        total = None
        for lq in range(2):
            for f in range(2):
                for h in range(2):
                    source = [params[0, lq, f, rows, 128 * c:128 * c + 128] for c in range(2)]
                    total = place(total, source, lq * 4 + f * 2 + h)
        strips[HALF // 2, rows] = total
        total = jnp.zeros((8, 128), F32)
        for f in range(2):
            source = [params[0, 2, f, rows, 128 * c:128 * c + 128] for c in range(2)]
            total = place(total, source, f * 2)
        strips[HALF // 2 + 1, rows] = total


def window_kernel(state, params, below, above, strips, strips_below, strips_above, weights, sides, strip_sides,
                  new_state, mean, edges, xa, xb, xe, ta, tb, te, par, coef, scoef, spar, package,
                  xhi, xlo, tsplit, beside, strip_beside):
    lane = lanes()
    span = ROWS + 2 * HALO

    rim = jnp.zeros((1, 128), F32)

    def fill(i, carry):
        for u in range(2):
            lev = i * 2 + u
            for f in range(2):
                for c in range(2):
                    cols = slice(128 * c, 128 * c + 128)
                    xa[f, lev, c, PAD:PAD + HALO] = below[f, lev, :, cols]
                    for ref in (xa, xb):
                        ref[f, lev, c, PAD - 1:PAD] = rim
                        ref[f, lev, c, PAD + span:PAD + span + 1] = rim
                    xa[f, lev, c, PAD + HALO:PAD + HALO + 8] = state[0, f, lev, 0:8, cols]
                    xa[f, lev, c, PAD + HALO + 8:PAD + HALO + 16] = state[0, f, lev, 8:16, cols]
                    xa[f, lev, c, PAD + HALO + 16:PAD + 2 * HALO + 16] = above[f, lev, :, cols]
        return carry

    lax.fori_loop(0, LEV // 2, fill, 0)
    for f in range(2):
        for kind in range(3):
            for c in range(2):
                cols = slice(128 * c, 128 * c + 128)
                par[kind, f, c, 0:HALO] = below[f, LEV + kind, :, cols]
                par[kind, f, c, HALO:HALO + 8] = params[0, kind, f, 0:8, cols]
                par[kind, f, c, HALO + 8:HALO + 16] = params[0, kind, f, 8:16, cols]
                par[kind, f, c, HALO + 16:2 * HALO + 16] = above[f, LEV + kind, :, cols]

    def unpack(dst, block, shift):
        dst[0:HALO] = pltpu.roll(strips_below[block], shift, 1)
        dst[HALO:HALO + 8] = pltpu.roll(strips[block, 0:8], shift, 1)
        dst[HALO + 8:HALO + 16] = pltpu.roll(strips[block, 8:16], shift, 1)
        dst[HALO + 16:2 * HALO + 16] = pltpu.roll(strips_above[block], shift, 1)

    def unstrip(block, carry):
        for lq in range(2):
            unpack(ta.at[block * 2 + lq, PAD:PAD + 24], block, 64 * lq)
            for ref in (ta, tb):
                ref[block * 2 + lq, PAD - 1:PAD] = rim
                ref[block * 2 + lq, PAD + span:PAD + span + 1] = rim
        return carry

    lax.fori_loop(0, HALF // 2, unstrip, 0)
    unpack(spar.at[0], HALF // 2, 0)
    unpack(spar.at[1], HALF // 2, 64)
    unpack(spar.at[2], HALF // 2 + 1, 0)

    columns = [(f, c, rt) for f in range(2) for c in range(2) for rt in range(TILES)]

    def mixing(value):
        return jnp.where(value > 0.0, value, 1.0)

    for f, c, rt in columns:
        rows = slice(8 * rt, 8 * rt + 8)
        k = mixing(par[1, f, c, rows])
        par[1, f, c, rows] = k
        par[3, f, c, rows] = 1.0 / k
        par[4, f, c, rows] = 1.0 - 4.0 * par[0, f, c, rows]
    for rt in range(TILES):
        rows = slice(8 * rt, 8 * rt + 8)
        k = mixing(spar[1, rows])
        spar[1, rows] = k
        spar[3, rows] = 1.0 / k
        spar[4, rows] = 1.0 - 4.0 * spar[0, rows]

    def pivots(level, carry):
        out = []
        for n, (f, c, rt) in enumerate(columns):
            rows = slice(8 * rt, 8 * rt + 8)
            k = par[1, f, c, rows]
            m = k / (1.0 + 2.0 * k - k * carry[n])
            coef[f, level, c, rows] = m
            out.append(m)
        for rt in range(TILES):
            rows = slice(8 * rt, 8 * rt + 8)
            k = spar[1, rows]
            m = k / (1.0 + 2.0 * k - k * carry[len(columns) + rt])
            scoef[level, rows] = m
            out.append(m)
        return tuple(out)

    one = jnp.ones((8, 128), F32)
    last = lax.fori_loop(0, HALF, pivots, (one,) * (len(columns) + TILES))
    for n, (f, c, rt) in enumerate(columns):
        coef[f, HALF, c, 8 * rt:8 * rt + 8] = last[n] / (1.0 - last[n] * last[n])
    for rt in range(TILES):
        m = last[len(columns) + rt]
        scoef[HALF, 8 * rt:8 * rt + 8] = m / (1.0 - m * m)

    def main_field(x, xn, f):
        for rt in range(TILES):
            rows = slice(8 * rt, 8 * rt + 8)
            at = PAD + 8 * rt
            diff = [par[0, f, c, rows] for c in range(2)]
            keep = [par[4, f, c, rows] for c in range(2)]

            def forward(i, carry):
                carry = list(carry)
                for u in range(4):
                    level = i * 4 + u
                    m = [coef[f, level, c, rows] for c in range(2)]
                    flat = pl.ds(pl.multiple_of(level * span, 8) + 8 * rt, 8)
                    for h in range(2):
                        lam = level if h == 0 else LEV - 1 - level
                        for c in range(2):
                            around = (
                                x[f, lam, c, at - 1:at + 7] + x[f, lam, c, at + 1:at + 9]
                            ) + beside[f, h, flat, 128 * c:128 * c + 128]
                            e = (keep[c] * x[f, lam, c, at:at + 8] + diff[c] * around) + carry[h * 2 + c]
                            xe[lam, c, rows] = e
                            carry[h * 2 + c] = m[c] * e
                return tuple(carry)

            zero = jnp.zeros((8, 128), F32)
            start = (par[2, f, 0, rows], par[2, f, 1, rows], zero, zero)
            ends = lax.fori_loop(0, HALF // 4, forward, start)
            inv = [par[3, f, c, rows] for c in range(2)]
            closing = [coef[f, HALF, c, rows] for c in range(2)]
            z = []
            for h in range(2):
                lam = HALF - 1 + h
                for c in range(2):
                    z.append(closing[c] * (xe[lam, c, rows] + ends[(1 - h) * 2 + c]))
            for h in range(2):
                for c in range(2):
                    xn[f, HALF - 1 + h, c, at:at + 8] = z[h * 2 + c] * inv[c]

            def back_level(level, z):
                out = []
                m = [coef[f, level, c, rows] for c in range(2)]
                for h in range(2):
                    lam = level if h == 0 else LEV - 1 - level
                    for c in range(2):
                        v = m[c] * (xe[lam, c, rows] + z[h * 2 + c])
                        xn[f, lam, c, at:at + 8] = v * inv[c]
                        out.append(v)
                return tuple(out)

            def back(i, z):
                for u in range(2):
                    z = back_level(HALF - 3 - (i * 2 + u) + 1, z)
                return z

            z = lax.fori_loop(0, HALF // 2 - 1, back, tuple(z))
            back_level(0, z)

    def strip_step(t, tn):
        diff = [spar[0, 8 * rt:8 * rt + 8] for rt in range(TILES)]
        keep = [spar[4, 8 * rt:8 * rt + 8] for rt in range(TILES)]
        inv = [spar[3, 8 * rt:8 * rt + 8] for rt in range(TILES)]

        def forward(i, carry):
            carry = list(carry)
            for u in range(2):
                level = i * 2 + u
                for rt in range(TILES):
                    at = PAD + 8 * rt
                    flat = pl.ds(pl.multiple_of(level * span, 8) + 8 * rt, 8)
                    around = (t[level, at - 1:at + 7] + t[level, at + 1:at + 9]) + strip_beside[flat]
                    e = (keep[rt] * t[level, at:at + 8] + diff[rt] * around) + carry[rt]
                    te[level, 8 * rt:8 * rt + 8] = e
                    carry[rt] = scoef[level, 8 * rt:8 * rt + 8] * e
            return tuple(carry)

        start = tuple(spar[2, 8 * rt:8 * rt + 8] for rt in range(TILES))
        ends = lax.fori_loop(0, HALF // 2, forward, start)
        z = []
        for rt in range(TILES):
            at = PAD + 8 * rt
            other = jnp.where((lane & 16) == 0, roll(ends[rt], -16), roll(ends[rt], 16))
            v = scoef[HALF, 8 * rt:8 * rt + 8] * (te[HALF - 1, 8 * rt:8 * rt + 8] + other)
            tn[HALF - 1, at:at + 8] = v * inv[rt]
            z.append(v)

        def back(i, z):
            level = HALF - 2 - i
            out = []
            for rt in range(TILES):
                at = PAD + 8 * rt
                v = scoef[level, 8 * rt:8 * rt + 8] * (te[level, 8 * rt:8 * rt + 8] + z[rt])
                tn[level, at:at + 8] = v * inv[rt]
                out.append(v)
            return tuple(out)

        lax.fori_loop(0, HALF - 1, back, tuple(z))

    places = [(c, rt) for c in range(2) for rt in range(2)]

    def level_of(level, h):
        return level if h == 0 else LEV - 1 - level

    def halves(value):
        high = value.astype(jnp.bfloat16)
        return high, (value - high.astype(F32)).astype(jnp.bfloat16)

    def split(x):
        def pair(i, carry):
            at = pl.ds(pl.multiple_of(i * 2 * span, 16), 2 * span)
            for f in range(2):
                for h in range(2):
                    for c in range(2):
                        value = jnp.concatenate(
                            [x[f, level_of(i * 2 + u, h), c, PAD:PAD + span] for u in range(2)], axis=0
                        )
                        high, low = halves(value)
                        xhi[f, h, at, 128 * c:128 * c + 128] = high
                        xlo[f, h, at, 128 * c:128 * c + 128] = low
            return carry

        lax.fori_loop(0, HALF // 2, pair, 0)

    def split_strip(t):
        def pair(i, carry):
            at = pl.ds(pl.multiple_of(i * 2 * span, 16), 2 * span)
            value = jnp.concatenate([t[i * 2 + u, PAD:PAD + span] for u in range(2)], axis=0)
            high, low = halves(value)
            tsplit[at, 0:128] = high
            tsplit[at, 128:256] = low
            return carry

        lax.fori_loop(0, HALF // 2, pair, 0)

    chunk = 256

    def neighbours():
        def part(i, carry):
            at = pl.ds(pl.multiple_of(i * chunk, 16), chunk)
            for f in range(2):
                for h in range(2):
                    value = jnp.concatenate([xhi[f, h, at], xlo[f, h, at], tsplit[at]], axis=1)
                    beside[f, h, at] = jnp.dot(value, sides[f, h], preferred_element_type=F32)
            strip_beside[at] = jnp.dot(tsplit[at], strip_sides[...], preferred_element_type=F32)
            return carry

        lax.fori_loop(0, HALF * span // chunk, part, 0)

    def packages():
        total = None
        for f in range(2):
            for h in range(2):
                both = jnp.dot(weights[f, h], xhi[f, h], preferred_element_type=F32)
                high = jnp.dot(weights[f, h, :NQ * ROWS], xlo[f, h], preferred_element_type=F32)
                value = (both[NQ * ROWS:] + high) + both[:NQ * ROWS]
                total = value if total is None else total + value
        package[...] = package[...] + jnp.tanh(total)

    package[...] = jnp.zeros_like(package)

    for step in range(STEPS):
        x, xn, t, tn = (xa, xb, ta, tb) if step % 2 == 0 else (xb, xa, tb, ta)
        split(x)
        split_strip(t)
        neighbours()
        if step > 0:
            packages()
        for f in range(2):
            main_field(x, xn, f)
        if step < STEPS - 1:
            strip_step(t, tn)
    split(xn)
    packages()

    def write(lev, carry):
        for f in range(2):
            for c in range(2):
                for rt in range(2):
                    at = PAD + HALO + 8 * rt
                    new_state[0, f, lev, 8 * rt:8 * rt + 8, 128 * c:128 * c + 128] = xn[f, lev, c, at:at + 8]
        return carry

    lax.fori_loop(0, LEV, write, 0)
    for rt in range(2):
        total = jnp.zeros((8, 128), F32)
        for q in range(NQ):
            at = q * ROWS + 8 * rt
            value = [package[at:at + 8, 128 * c:128 * c + 128] * (1.0 / STEPS) for c in range(2)]
            for c in range(2):
                mean[q, 8 * rt:8 * rt + 8, 128 * c:128 * c + 128] = value[c]
            ring = jnp.where(lane >= 126, value[1], value[0])
            total = jnp.where((lane >= 4 * q) & (lane < 4 * q + 4), roll(ring, 4 * q + 2), total)
        edges[8 * rt:8 * rt + 8] = total


def remap_kernel(table, received, west_edges, east_edges, codes, mask, out):
    lane = lanes()
    for rt in range(2):
        rows = slice(8 * rt, 8 * rt + 8)
        west_edge = west_edges[rows]
        east_edge = east_edges[rows]
        picks, first, second, sea = [], [], [], []
        for c in range(2):
            cols = slice(128 * c, 128 * c + 128)
            code = codes[0, rows, cols]
            offset = code & 3
            row = code >> 2
            w = []
            for j in range(2):
                v = jnp.full((8, 128), table[0, 0, j], F32)
                for n in range(1, 4):
                    v = jnp.where(row == n, table[0, n, j], v)
                w.append(v)
            first.append(w[0])
            second.append(w[1])
            picks.append([offset == n for n in range(1, 4)])
            sea.append(mask[0, rows, cols] == 1)
        for q in range(NQ):
            v = [received[q, rows, 128 * c:128 * c + 128] for c in range(2)]
            shifted = [[None] * 5, [None] * 5]
            for c in range(2):
                shifted[c][2] = v[c]
            for d in (1, 2):
                turned = [roll(u, d) for u in v]
                far = roll(west_edge, d - (4 * q + 2))
                shifted[0][2 - d] = jnp.where(lane < d, far, turned[0])
                shifted[1][2 - d] = jnp.where(lane < d, turned[0], turned[1])
                turned = [roll(u, -d) for u in v]
                far = roll(east_edge, 128 - d - (4 * q + 2))
                shifted[0][2 + d] = jnp.where(lane >= 128 - d, turned[1], turned[0])
                shifted[1][2 + d] = jnp.where(lane >= 128 - d, far, turned[1])
            for c in range(2):
                near, beyond = shifted[c][0], shifted[c][1]
                for n in range(1, 4):
                    near = jnp.where(picks[c][n - 1], shifted[c][n], near)
                    beyond = jnp.where(picks[c][n - 1], shifted[c][n + 1], beyond)
                value = first[c] * near + second[c] * beyond
                out[0, q, rows, 128 * c:128 * c + 128] = jnp.where(sea[c], value, 0.0)


def matrices_kernel(couple_weight, weights, sides, strip_sides):
    span = ROWS + 2 * HALO
    width = HALF * span
    level = lax.broadcasted_iota(jnp.int32, (LEV, width), 0)
    place = lax.broadcasted_iota(jnp.int32, (LEV, width), 1)
    spread = []
    for h in range(2):
        first = span * (level if h == 0 else LEV - 1 - level)
        spread.append(((place >= first) & (place < first + span)).astype(F32).astype(jnp.bfloat16))
    count = lax.broadcasted_iota(jnp.int32, (8, LEV), 1).astype(F32).astype(jnp.bfloat16)
    block = jnp.dot(count, spread[0], preferred_element_type=F32)[0:1].astype(jnp.int32)
    row = lax.broadcasted_iota(jnp.int32, (ROWS, width), 0)
    within = lax.broadcasted_iota(jnp.int32, (ROWS, width), 1) - span * block
    keep = within == row + HALO
    for f in range(2):
        value = couple_weight[0, :, f, :]
        high = value.astype(jnp.bfloat16)
        low = (value - high.astype(F32)).astype(jnp.bfloat16)
        for h in range(2):
            for n, part in enumerate((high, low)):
                wide = jnp.dot(part, spread[h], preferred_element_type=F32)
                for q in range(NQ):
                    at = n * NQ * ROWS + q * ROWS
                    weights[f, h, at:at + ROWS] = jnp.where(keep, wide[q:q + 1], 0.0).astype(jnp.bfloat16)
    row = lax.broadcasted_iota(jnp.int32, (COLS, COLS), 0)
    col = lax.broadcasted_iota(jnp.int32, (COLS, COLS), 1)
    inner = (jnp.abs(row - col) == 1).astype(F32).astype(jnp.bfloat16)
    lane = row & 127
    for f in range(2):
        for h in range(2):
            base = f * 32 + h * 16
            rim = ((lane == base + 3) & (col == 0)) | ((lane == base + 12) & (col == COLS - 1))
            sides[f, h, 0:COLS] = inner
            sides[f, h, COLS:2 * COLS] = inner
            sides[f, h, 2 * COLS:3 * COLS] = rim.astype(F32).astype(jnp.bfloat16)
    near = jnp.abs((row & 127) - col)[:, 0:128] == 1
    strip_sides[...] = near.astype(F32).astype(jnp.bfloat16)


def matrices(couple_weight):
    return pl.pallas_call(
        matrices_kernel,
        out_shape=(
            jax.ShapeDtypeStruct((2, 2, 2 * NQ * ROWS, FLAT), jnp.bfloat16),
            jax.ShapeDtypeStruct((2, 2, 3 * COLS, COLS), jnp.bfloat16),
            jax.ShapeDtypeStruct((256, 128), jnp.bfloat16),
        ),
        in_specs=[VMEM],
        out_specs=[VMEM] * 3,
        compiler_params=pltpu.CompilerParams(vmem_limit_bytes=50 * 2**20),
        name="matrices",
    )(couple_weight)


def ring(count, step, periodic):
    pairs = [(i, i + step) for i in range(count)]
    if periodic:
        return [(a, b % count) for a, b in pairs]
    return [(a, b) for a, b in pairs if 0 <= b < count]


def window(*args):
    return pl.pallas_call(
        window_kernel,
        out_shape=(
            jax.ShapeDtypeStruct((1, 2, LEV, ROWS, COLS), F32),
            jax.ShapeDtypeStruct((NQ, ROWS, COLS), F32),
            jax.ShapeDtypeStruct((ROWS, 128), F32),
        ),
        in_specs=[VMEM] * 10,
        out_specs=[VMEM] * 3,
        scratch_shapes=[
            pltpu.VMEM((2, LEV, 2, TALL, 128), F32),
            pltpu.VMEM((2, LEV, 2, TALL, 128), F32),
            pltpu.VMEM((LEV, 2, 24, 128), F32),
            pltpu.VMEM((HALF, TALL, 128), F32),
            pltpu.VMEM((HALF, TALL, 128), F32),
            pltpu.VMEM((HALF, 24, 128), F32),
            pltpu.VMEM((5, 2, 2, 24, 128), F32),
            pltpu.VMEM((2, HALF + 1, 2, 24, 128), F32),
            pltpu.VMEM((HALF + 1, 24, 128), F32),
            pltpu.VMEM((5, 24, 128), F32),
            pltpu.VMEM((NQ * ROWS, COLS), F32),
            pltpu.VMEM((2, 2, FLAT, COLS), jnp.bfloat16),
            pltpu.VMEM((2, 2, FLAT, COLS), jnp.bfloat16),
            pltpu.VMEM((FLAT, 256), jnp.bfloat16),
            pltpu.VMEM((2, 2, FLAT, COLS), F32),
            pltpu.VMEM((FLAT, 128), F32),
        ],
        compiler_params=pltpu.CompilerParams(vmem_limit_bytes=50 * 2**20),
        name="window",
    )(*args)


def local(state, params, couple_weight, weight_table, intersection_map, sea_mask):
    lon, lat = lax.axis_size("lon"), lax.axis_size("lat")
    limit = pltpu.CompilerParams(vmem_limit_bytes=50 * 2**20)
    low_rows, high_rows, strips = pl.pallas_call(
        pack_kernel,
        out_shape=(
            jax.ShapeDtypeStruct((2, PLANES, HALO, COLS), F32),
            jax.ShapeDtypeStruct((2, PLANES, HALO, COLS), F32),
            jax.ShapeDtypeStruct((STRIPS, ROWS, 128), F32),
        ),
        in_specs=[VMEM] * 2,
        out_specs=[VMEM] * 3,
        compiler_params=limit,
        name="pack",
    )(state, params)
    below = lax.ppermute(high_rows, "lat", ring(lat, 1, False))
    above = lax.ppermute(low_rows, "lat", ring(lat, -1, False))
    west = lax.ppermute(strips, "lon", ring(lon, 1, True))
    east = lax.ppermute(strips, "lon", ring(lon, -1, True))
    place = jnp.arange(128, dtype=jnp.int32) % 16
    strips = jnp.where(place < 4, west, jnp.where(place >= 12, east, strips))
    strips_below = lax.ppermute(strips[:, ROWS - HALO:], "lat", ring(lat, 1, False))
    strips_above = lax.ppermute(strips[:, :HALO], "lat", ring(lat, -1, False))
    weights, sides, strip_sides = matrices(couple_weight)
    new_state, mean, edges = window(
        state, params, below, above, strips, strips_below, strips_above, weights, sides, strip_sides
    )
    received = lax.ppermute(mean, "comp", [(0, 1), (1, 0)])

    def across(step):
        return [(a * 2 + s, b * 2 + 1 - s) for a, b in ring(lon, step, True) for s in range(2)]

    west_edges = lax.ppermute(edges, ("lon", "comp"), across(1))
    east_edges = lax.ppermute(edges, ("lon", "comp"), across(-1))
    coupled = pl.pallas_call(
        remap_kernel,
        out_shape=jax.ShapeDtypeStruct((1, NQ, ROWS, COLS), F32),
        in_specs=[SMEM] + [VMEM] * 5,
        out_specs=VMEM,
        compiler_params=limit,
        name="remap",
    )(weight_table, received, west_edges, east_edges, intersection_map, sea_mask)
    return new_state, coupled


def solution(mesh):
    placed = (
        P("comp", None, None, "lat", "lon"),
        P("comp", None, None, "lat", "lon"),
        P("comp", None, None, None),
        P("comp", None, None),
        P("comp", "lat", "lon"),
        P("comp", "lat", "lon"),
    )
    return jax.shard_map(
        local,
        mesh=mesh,
        in_specs=placed,
        out_specs=(P("comp", None, None, "lat", "lon"), P("comp", None, "lat", "lon")),
        check_vma=False,
    )
```

```python
import jax
import jax.numpy as jnp
from jax import lax
from jax.experimental import pallas as pl
from jax.experimental.pallas import tpu as pltpu
from jax.sharding import PartitionSpec as P

STEPS = 4
LEV = 64
HALF = LEV // 2
ROWS = 16
HALO = 4
COLS = 256
NQ = 8
OFF = 8
TALL = 32
PLANES = LEV + 3
STRIPS = HALF // 2 + 2
VMEM = pl.BlockSpec(memory_space=pltpu.VMEM)
SMEM = pl.BlockSpec(memory_space=pltpu.SMEM)
HBM = pl.BlockSpec(memory_space=pltpu.HBM)
BF16 = jnp.bfloat16
F32 = jnp.float32


def lanes():
    return lax.broadcasted_iota(jnp.int32, (8, 128), 1)


def subs():
    return lax.broadcasted_iota(jnp.int32, (8, 128), 0)


def level_of(level, h):
    return level if h == 0 else LEV - 1 - level


def halves(value):
    high = value.astype(BF16)
    return high, (value - high.astype(F32)).astype(BF16)


def params_of(vmem):
    return pltpu.CompilerParams(vmem_limit_bytes=vmem * 2**20)


def roll(value, shift):
    return pltpu.roll(value, shift % 128, 1)


def load_kernel(state, params, x0, strips, near, sem, near_sem):
    lane = lanes()
    part = LEV // 4
    copies = {}
    for n in (0, 3, 1, 2):
        for f in range(2):
            for c in range(2):
                copies[n, f, c] = pltpu.make_async_copy(
                    state.at[0, f, pl.ds(part * n, part), :, pl.ds(128 * c, 128)],
                    x0.at[f, pl.ds(part * n, part), c, pl.ds(OFF, ROWS)],
                    sem.at[n, f, c],
                )
                copies[n, f, c].start()
    small = pltpu.make_async_copy(params.at[0], near, near_sem)
    small.start()

    def place(total, source, index):
        ring = jnp.where(lane >= 124, source[1], source[0])
        first = roll(ring, 16 * index + 4)
        second = roll(ring, 16 * index + 12)
        inside = (lane >= 16 * index) & (lane < 16 * index + 16)
        pair = jnp.where((lane & 8) == 0, first, second)
        return pair if total is None else jnp.where(inside, pair, total)

    def strip(block, carry):
        for rt in range(2):
            at = OFF + 8 * rt
            total = None
            for lq in range(2):
                for f in range(2):
                    for h in range(2):
                        lam = level_of(block * 2 + lq, h)
                        source = [x0[f, lam, c, at:at + 8] for c in range(2)]
                        total = place(total, source, lq * 4 + f * 2 + h)
            strips[block, 8 * rt:8 * rt + 8] = total
        return carry

    for n in range(2):
        for m in (n, 3 - n):
            for f in range(2):
                for c in range(2):
                    copies[m, f, c].wait()
        lax.fori_loop(n * part // 2, (n + 1) * part // 2, strip, 0)
    small.wait()
    for rt in range(2):
        rows = slice(8 * rt, 8 * rt + 8)
        total = None
        for lq in range(2):
            for f in range(2):
                for h in range(2):
                    source = [near[lq, f, rows, 128 * c:128 * c + 128] for c in range(2)]
                    total = place(total, source, lq * 4 + f * 2 + h)
        strips[HALF // 2, rows] = total
        total = jnp.zeros((8, 128), F32)
        for f in range(2):
            source = [near[2, f, rows, 128 * c:128 * c + 128] for c in range(2)]
            total = place(total, source, f * 2)
        strips[HALF // 2 + 1, rows] = total


def join_kernel(strips, west, east, low_in, high_in, joined, low_rows, high_rows):
    place = lanes() & 15
    for block in range(STRIPS):
        for rt in range(2):
            rows = slice(8 * rt, 8 * rt + 8)
            joined[block, rows] = jnp.where(
                place < 4, west[block, rows], jnp.where(place >= 12, east[block, rows], strips[block, rows])
            )
        cols = slice(128 * (block % 2), 128 * (block % 2) + 128)
        low_rows[2 * PLANES + block // 2, :, cols] = joined[block, 0:HALO]
        high_rows[2 * PLANES + block // 2, :, cols] = joined[block, ROWS - HALO:ROWS]


def kron_weights(couple_weight, out, rows):
    width = HALF * rows
    level = lax.broadcasted_iota(jnp.int32, (LEV, width), 0)
    place = lax.broadcasted_iota(jnp.int32, (LEV, width), 1)
    spread = []
    for h in range(2):
        first = rows * level_of(level, h)
        spread.append(((place >= first) & (place < first + rows)).astype(F32).astype(BF16))
    row = lax.broadcasted_iota(jnp.int32, (rows, width), 0)
    within = lax.broadcasted_iota(jnp.int32, (rows, width), 1) & (rows - 1)
    keep = within == row
    for f in range(2):
        for n, part in enumerate(halves(couple_weight[0, :, f, :])):
            for h in range(2):
                wide = jnp.dot(part, spread[h], preferred_element_type=F32)
                for q in range(0, NQ, 2):
                    at = n * NQ * rows + q * rows
                    pair = [jnp.where(keep, wide[q + i:q + i + 1], 0.0) for i in range(2)]
                    out[f, h, at:at + 2 * rows] = jnp.concatenate(pair, axis=0).astype(BF16)


def prepare_kernel(x0, params, couple_weight,
                   low_rows, high_rows, weights, narrow, sides, strip_sides, par, coef, xhi, xlo):
    def some(level, carry):
        at = pl.ds(pl.multiple_of(level * ROWS, 16), ROWS)
        for f in range(2):
            for h in range(2):
                lam = level_of(level, h)
                for c in range(2):
                    cols = slice(128 * c, 128 * c + 128)
                    value = x0[f, lam, c, OFF:OFF + ROWS]
                    high, low = halves(value)
                    xhi[f, h, at, cols] = high
                    xlo[f, h, at, cols] = low
                    low_rows[f * PLANES + lam, :, cols] = x0[f, lam, c, OFF:OFF + HALO]
                    high_rows[f * PLANES + lam, :, cols] = x0[f, lam, c, OFF + ROWS - HALO:OFF + ROWS]
        return carry

    for f in range(2):
        for kind in range(3):
            low_rows[f * PLANES + LEV + kind] = params[0, kind, f, 0:HALO]
            high_rows[f * PLANES + LEV + kind] = params[0, kind, f, ROWS - HALO:ROWS]
    columns = [(f, c, rt) for f in range(2) for c in range(2) for rt in range(2)]
    for f, c, rt in columns:
        rows = slice(8 * rt, 8 * rt + 8)
        h, k, g = [params[0, kind, f, rows, 128 * c:128 * c + 128] for kind in range(3)]
        for n, value in enumerate((h, k, g, 1.0 / k, 1.0 - 4.0 * h)):
            par[n, f, c, rows] = value

    def pivots(level, carry):
        out = []
        for n, (f, c, rt) in enumerate(columns):
            rows = slice(8 * rt, 8 * rt + 8)
            k = par[1, f, c, rows]
            m = k / (1.0 + 2.0 * k - k * carry[n])
            coef[f, level, c, rows] = m
            out.append(m)
        some(level, 0)
        return tuple(out)

    last = lax.fori_loop(0, HALF, pivots, (jnp.ones((8, 128), F32),) * len(columns))
    for n, (f, c, rt) in enumerate(columns):
        coef[f, HALF, c, 8 * rt:8 * rt + 8] = last[n] / (1.0 - last[n] * last[n])
    kron_weights(couple_weight, weights, ROWS)
    kron_weights(couple_weight, narrow, 8)
    row = lax.broadcasted_iota(jnp.int32, (COLS, COLS), 0)
    col = lax.broadcasted_iota(jnp.int32, (COLS, COLS), 1)
    inner = (jnp.abs(row - col) == 1).astype(F32).astype(jnp.bfloat16)
    lane = row & 127
    for f in range(2):
        for h in range(2):
            base = f * 32 + h * 16
            rim = ((lane == base + 3) & (col == 0)) | ((lane == base + 12) & (col == COLS - 1))
            sides[f, h, 0:COLS] = inner
            sides[f, h, COLS:2 * COLS] = inner
            sides[f, h, 2 * COLS:3 * COLS] = rim.astype(F32).astype(jnp.bfloat16)
    near = jnp.abs((row & 127) - col)[:, 0:128] == 1
    strip_sides[...] = near.astype(F32).astype(jnp.bfloat16)

def strip_params(spar):
    for rt in range(2):
        rows = slice(8 * rt, 8 * rt + 8)
        k = spar[1, rows]
        k = jnp.where(k > 0.0, k, 1.0)
        spar[1, rows] = k
        spar[3, rows] = 1.0 / k
        spar[4, rows] = 1.0 - 4.0 * spar[0, rows]


def strip_pivots(spar, scoef, level, carry):
    out = []
    for rt in range(2):
        rows = slice(8 * rt, 8 * rt + 8)
        k = spar[1, rows]
        m = k / (1.0 + 2.0 * k - k * carry[rt])
        scoef[level, rows] = m
        out.append(m)
    return tuple(out)


def strip_closing(scoef, last):
    for rt in range(2):
        scoef[HALF, 8 * rt:8 * rt + 8] = last[rt] / (1.0 - last[rt] * last[rt])


def swap_ends(value):
    return jnp.where((lanes() & 16) == 0, roll(value, -16), roll(value, 16))


def inner_kernel(strips, x0_in, xhi_in, xlo_in, par, coef, weights, sides, strip_sides,
                 x0, xhi, xlo, x1, x2, x3, x4, t0, t1, t2, t3, sums,
                 xe, te, spar, scoef, tsplit, beside, strip_beside):
    xs, ts = (x0, x1, x2, x3, x4), (t0, t1, t2, t3)
    sub = subs()
    zero = jnp.zeros((8, 128), F32)

    for rt in range(2):
        rows = slice(8 * rt, 8 * rt + 8)
        spar[0, rows] = strips[HALF // 2, rows]
        spar[1, rows] = roll(strips[HALF // 2, rows], 64)
        spar[2, rows] = strips[HALF // 2 + 1, rows]
    strip_params(spar)

    def unstrip(block, carry):
        for lq in range(2):
            level = block * 2 + lq
            tiles = [roll(strips[block, 8 * rt:8 * rt + 8], 64 * lq) for rt in range(2)]
            for rt in range(2):
                t0[level, OFF + 8 * rt:OFF + 8 * rt + 8] = tiles[rt]
            split_strip(level, tiles)
            carry = strip_pivots(spar, scoef, level, carry)
        return carry

    def split_strip(level, tiles):
        at = pl.ds(pl.multiple_of(level * ROWS, 16), ROWS)
        high, low = halves(jnp.concatenate(tiles, axis=0))
        tsplit[at, 0:128] = high
        tsplit[at, 128:256] = low

    one = jnp.ones((8, 128), F32)
    strip_closing(scoef, lax.fori_loop(0, HALF // 2, unstrip, (one, one)))

    def vertical(load, rt):
        at = OFF + 8 * rt
        up, down = load(at - 1), load(at + 1)
        if rt == 0:
            up = jnp.where(sub == 0, 0.0, up)
        else:
            down = jnp.where(sub == 7, 0.0, down)
        return up + down

    def neighbours():
        def part(i, carry):
            at = pl.ds(pl.multiple_of(i * 256, 16), 256)
            for f in range(2):
                for h in range(2):
                    value = jnp.concatenate([xhi[f, h, at], xlo[f, h, at], tsplit[at]], axis=1)
                    beside[f, h, at] = jnp.dot(value, sides[f, h], preferred_element_type=F32)
            strip_beside[at] = jnp.dot(tsplit[at], strip_sides[...], preferred_element_type=F32)
            return carry

        lax.fori_loop(0, HALF * ROWS // 256, part, 0)

    def packages(n):
        total = None
        for f in range(2):
            for h in range(2):
                both = jnp.dot(weights[f, h], xhi[f, h], preferred_element_type=F32)
                high = jnp.dot(weights[f, h, :NQ * ROWS], xlo[f, h], preferred_element_type=F32)
                value = (both[NQ * ROWS:] + high) + both[:NQ * ROWS]
                total = value if total is None else total + value
        sums[n] = total

    def main_field(x, xn, f):
        tiles = [(c, rt, slice(8 * rt, 8 * rt + 8), OFF + 8 * rt) for c in range(2) for rt in range(2)]
        diff = [par[0, f, c, rows] for c, rt, rows, at in tiles]
        keep = [par[4, f, c, rows] for c, rt, rows, at in tiles]

        def forward(i, carry):
            carry = list(carry)
            for u in range(2):
                level = i * 2 + u
                for n, (c, rt, rows, at) in enumerate(tiles):
                    m = coef[f, level, c, rows]
                    flat = pl.ds(pl.multiple_of(level * ROWS, 8) + 8 * rt, 8)
                    for h in range(2):
                        lam = level_of(level, h)
                        around = vertical(lambda r: x[f, lam, c, r:r + 8], rt)
                        around = around + beside[f, h, flat, 128 * c:128 * c + 128]
                        e = (keep[n] * x[f, lam, c, at:at + 8] + diff[n] * around) + carry[h * 4 + n]
                        xe[lam, c, rows] = e
                        carry[h * 4 + n] = m * e
            return tuple(carry)

        start = tuple(par[2, f, c, rows] for c, rt, rows, at in tiles) + (zero,) * 4
        ends = lax.fori_loop(0, HALF // 2, forward, start)
        inv = [par[3, f, c, rows] for c, rt, rows, at in tiles]

        def finish(level, h, z):
            lam = level_of(level, h)
            flat = pl.ds(pl.multiple_of(level * ROWS, 16), ROWS)
            for c in range(2):
                y = []
                for rt in range(2):
                    v = z[h * 4 + 2 * c + rt] * inv[2 * c + rt]
                    xn[f, lam, c, OFF + 8 * rt:OFF + 8 * rt + 8] = v
                    y.append(v)
                high, low = halves(jnp.concatenate(y, axis=0))
                xhi[f, h, flat, 128 * c:128 * c + 128] = high
                xlo[f, h, flat, 128 * c:128 * c + 128] = low

        z = [None] * 8
        for h in range(2):
            for n, (c, rt, rows, at) in enumerate(tiles):
                z[h * 4 + n] = coef[f, HALF, c, rows] * (xe[HALF - 1 + h, c, rows] + ends[(1 - h) * 4 + n])
        for h in range(2):
            finish(HALF - 1, h, z)

        def back_level(level, z):
            out = [None] * 8
            for h in range(2):
                lam = level_of(level, h)
                for n, (c, rt, rows, at) in enumerate(tiles):
                    out[h * 4 + n] = coef[f, level, c, rows] * (xe[lam, c, rows] + z[h * 4 + n])
                finish(level, h, out)
            return tuple(out)

        def back(i, z):
            for u in range(3):
                z = back_level(HALF - 2 - (i * 3 + u), z)
            return z

        z = lax.fori_loop(0, HALF // 3, back, tuple(z))
        back_level(0, z)

    def strip_step(t, tn):
        tiles = [slice(8 * rt, 8 * rt + 8) for rt in range(2)]
        diff = [spar[0, rows] for rows in tiles]
        inv = [spar[3, rows] for rows in tiles]
        keep = [spar[4, rows] for rows in tiles]

        def forward(i, carry):
            carry = list(carry)
            for u in range(4):
                level = i * 4 + u
                for rt, rows in enumerate(tiles):
                    flat = pl.ds(pl.multiple_of(level * ROWS, 8) + 8 * rt, 8)
                    around = vertical(lambda r: t[level, r:r + 8], rt) + strip_beside[flat]
                    e = (keep[rt] * t[level, OFF + 8 * rt:OFF + 8 * rt + 8] + diff[rt] * around) + carry[rt]
                    te[level, rows] = e
                    carry[rt] = scoef[level, rows] * e
            return tuple(carry)

        ends = lax.fori_loop(0, HALF // 4, forward, tuple(spar[2, rows] for rows in tiles))
        def finish(level, z):
            y = [z[rt] * inv[rt] for rt in range(2)]
            for rt in range(2):
                tn[level, OFF + 8 * rt:OFF + 8 * rt + 8] = y[rt]
            split_strip(level, y)

        z = [scoef[HALF, rows] * (te[HALF - 1, rows] + swap_ends(ends[rt])) for rt, rows in enumerate(tiles)]
        finish(HALF - 1, z)

        def back_level(level, z):
            out = [scoef[level, rows] * (te[level, rows] + z[rt]) for rt, rows in enumerate(tiles)]
            finish(level, out)
            return tuple(out)

        def back(i, z):
            for u in range(3):
                z = back_level(HALF - 2 - (i * 3 + u), z)
            return z

        z = lax.fori_loop(0, HALF // 3, back, tuple(z))
        back_level(0, z)

    for step in range(STEPS):
        neighbours()
        if step > 0:
            packages(step - 1)
        for f in range(2):
            main_field(xs[step], xs[step + 1], f)
        if step < STEPS - 1:
            strip_step(ts[step], ts[step + 1])
    packages(STEPS - 1)


def outer_kernel(below, above, strips, params, sums, narrow, sides, strip_sides,
                 i0, i1, i2, i3, i4, j0, j1, j2, j3,
                 new_state, mean, edges, x0, x1, x2, x3, x4, t0, t1, t2, t3,
                 xe, te, par, coef, spar, scoef, centre, xhi, xlo, tcentre, tsplit, beside, strip_beside, patch, sem):
    xs, ts = (x0, x1, x2, x3, x4), (t0, t1, t2, t3)
    lane, sub = lanes(), subs()
    top = sub < 4
    zero = jnp.zeros((8, 128), F32)

    def strip_rim(ref, block):
        return ref[2 * PLANES + block // 2, :, 128 * (block % 2):128 * (block % 2) + 128]

    for n, (block, shift) in enumerate(((HALF // 2, 0), (HALF // 2, 64), (HALF // 2 + 1, 0))):
        spar[n, 0:4] = pltpu.roll(strip_rim(below, block), shift, 1)
        spar[n, 4:8] = pltpu.roll(strips[block, 0:4], shift, 1)
        spar[n, 8:12] = pltpu.roll(strips[block, 12:16], shift, 1)
        spar[n, 12:16] = pltpu.roll(strip_rim(above, block), shift, 1)
    strip_params(spar)
    columns = [(f, c, rt) for f in range(2) for c in range(2) for rt in range(2)]
    for f in range(2):
        for c in range(2):
            cols = slice(128 * c, 128 * c + 128)
            for n in range(3):
                par[n, f, c, 0:4] = below[f * PLANES + LEV + n, :, cols]
                par[n, f, c, 4:8] = params[0, n, f, 0:4, cols]
                par[n, f, c, 8:12] = params[0, n, f, 12:16, cols]
                par[n, f, c, 12:16] = above[f * PLANES + LEV + n, :, cols]
    for f, c, rt in columns:
        rows = slice(8 * rt, 8 * rt + 8)
        k = par[1, f, c, rows]
        k = jnp.where(k > 0.0, k, 1.0)
        par[1, f, c, rows] = k
        par[3, f, c, rows] = 1.0 / k
        par[4, f, c, rows] = 1.0 - 4.0 * par[0, f, c, rows]

    def pivots(level, carry):
        out = []
        for n, (f, c, rt) in enumerate(columns):
            rows = slice(8 * rt, 8 * rt + 8)
            k = par[1, f, c, rows]
            m = k / (1.0 + 2.0 * k - k * carry[n])
            coef[f, level, c, rows] = m
            out.append(m)
        out.extend(strip_pivots(spar, scoef, level, carry[len(columns):]))
        for f in range(2):
            for h in range(2):
                lam = level_of(level, h)
                for c in range(2):
                    cols = slice(128 * c, 128 * c + 128)
                    x0[f, lam, c, OFF - HALO:OFF] = below[f * PLANES + lam, :, cols]
                    x0[f, lam, c, OFF + ROWS:OFF + ROWS + HALO] = above[f * PLANES + lam, :, cols]
        return tuple(out)

    last = lax.fori_loop(0, HALF, pivots, (jnp.ones((8, 128), F32),) * (len(columns) + 2))
    for n, (f, c, rt) in enumerate(columns):
        coef[f, HALF, c, 8 * rt:8 * rt + 8] = last[n] / (1.0 - last[n] * last[n])
    strip_closing(scoef, last[len(columns):])

    def unstrip(i, carry):
        for c in range(2):
            cols = slice(128 * c, 128 * c + 128)
            for lq in range(2):
                level = i * 4 + c * 2 + lq
                t0[level, OFF - HALO:OFF] = pltpu.roll(below[2 * PLANES + i, :, cols], 64 * lq, 1)
                t0[level, OFF + ROWS:OFF + ROWS + HALO] = pltpu.roll(above[2 * PLANES + i, :, cols], 64 * lq, 1)
        return carry

    lax.fori_loop(0, HALF // 4, unstrip, 0)

    def gather(x, step):
        a, b = OFF - 4 + step, OFF + 12 - step

        def some(i, carry):
            at = pl.ds(pl.multiple_of(i * 16, 16), 16)
            for f in range(2):
                for h in range(2):
                    for c in range(2):
                        pair = []
                        for u in range(2):
                            lam = level_of(i * 2 + u, h)
                            v = jnp.where(top, x[f, lam, c, a:a + 8], x[f, lam, c, b:b + 8])
                            centre[f, lam, c] = v
                            pair.append(v)
                        high, low = halves(jnp.concatenate(pair, axis=0))
                        xhi[f, h, at, 128 * c:128 * c + 128] = high
                        xlo[f, h, at, 128 * c:128 * c + 128] = low
            return carry

        lax.fori_loop(0, HALF // 2, some, 0)

    def gather_strip(t, step):
        a, b = OFF - 4 + step, OFF + 12 - step

        def some(i, carry):
            at = pl.ds(pl.multiple_of(i * 16, 16), 16)
            pair = []
            for u in range(2):
                v = jnp.where(top, t[i * 2 + u, a:a + 8], t[i * 2 + u, b:b + 8])
                tcentre[i * 2 + u] = v
                pair.append(v)
            high, low = halves(jnp.concatenate(pair, axis=0))
            tsplit[at, 0:128] = high
            tsplit[at, 128:256] = low
            return carry

        lax.fori_loop(0, HALF // 2, some, 0)

    def neighbours():
        for f in range(2):
            for h in range(2):
                value = jnp.concatenate([xhi[f, h], xlo[f, h], tsplit[...]], axis=1)
                beside[f, h] = jnp.dot(value, sides[f, h], preferred_element_type=F32)
        strip_beside[...] = jnp.dot(tsplit[...], strip_sides[...], preferred_element_type=F32)

    def packages(n, step):
        a, b = OFF - 4 + step, OFF + 12 - step
        total = None
        for f in range(2):
            for h in range(2):
                both = jnp.dot(narrow[f, h], xhi[f, h], preferred_element_type=F32)
                high = jnp.dot(narrow[f, h, :NQ * 8], xlo[f, h], preferred_element_type=F32)
                value = (both[NQ * 8:] + high) + both[:NQ * 8]
                total = value if total is None else total + value
        for q in range(NQ):
            for c in range(2):
                v = total[q * 8:q * 8 + 8, 128 * c:128 * c + 128]
                pltpu.store(patch.at[n, q, c, pl.ds(a, 8)], v, mask=top)
                pltpu.store(patch.at[n, q, c, pl.ds(b, 8)], v, mask=sub >= 4)

    def main_field(x, xn, f, step):
        a, b = OFF - 4 + step, OFF + 12 - step

        def mine(load):
            return jnp.where(top, load(slice(step, step + 8)), load(slice(8 - step, 16 - step)))

        def put(lam, c, v):
            pltpu.store(xn.at[f, lam, c, pl.ds(a, 8)], v, mask=top)
            pltpu.store(xn.at[f, lam, c, pl.ds(b, 8)], v, mask=sub >= 4)

        diff = [mine(lambda r: par[0, f, c, r]) for c in range(2)]
        keep = [mine(lambda r: par[4, f, c, r]) for c in range(2)]
        inv = [mine(lambda r: par[3, f, c, r]) for c in range(2)]

        def forward(i, carry):
            carry = list(carry)
            for u in range(4):
                level = i * 4 + u
                m = [mine(lambda r: coef[f, level, c, r]) for c in range(2)]
                flat = pl.ds(pl.multiple_of(level * 8, 8), 8)
                for h in range(2):
                    lam = level_of(level, h)
                    for c in range(2):
                        around = jnp.where(
                            top,
                            x[f, lam, c, a - 1:a + 7] + x[f, lam, c, a + 1:a + 9],
                            x[f, lam, c, b - 1:b + 7] + x[f, lam, c, b + 1:b + 9],
                        ) + beside[f, h, flat, 128 * c:128 * c + 128]
                        e = (keep[c] * centre[f, lam, c] + diff[c] * around) + carry[h * 2 + c]
                        xe[lam, c] = e
                        carry[h * 2 + c] = m[c] * e
            return tuple(carry)

        start = (mine(lambda r: par[2, f, 0, r]), mine(lambda r: par[2, f, 1, r]), zero, zero)
        ends = lax.fori_loop(0, HALF // 4, forward, start)
        z = []
        for h in range(2):
            for c in range(2):
                v = mine(lambda r: coef[f, HALF, c, r]) * (xe[HALF - 1 + h, c] + ends[(1 - h) * 2 + c])
                put(HALF - 1 + h, c, v * inv[c])
                z.append(v)

        def back_level(level, z):
            out = []
            m = [mine(lambda r: coef[f, level, c, r]) for c in range(2)]
            for h in range(2):
                lam = level_of(level, h)
                for c in range(2):
                    v = m[c] * (xe[lam, c] + z[h * 2 + c])
                    put(lam, c, v * inv[c])
                    out.append(v)
            return tuple(out)

        def back(i, z):
            for u in range(3):
                z = back_level(HALF - 2 - (i * 3 + u), z)
            return z

        z = lax.fori_loop(0, HALF // 3, back, tuple(z))
        back_level(0, z)

    def strip_step(t, tn, step):
        a, b = OFF - 4 + step, OFF + 12 - step

        def mine(load):
            return jnp.where(top, load(slice(step, step + 8)), load(slice(8 - step, 16 - step)))

        def put(level, v):
            pltpu.store(tn.at[level, pl.ds(a, 8)], v, mask=top)
            pltpu.store(tn.at[level, pl.ds(b, 8)], v, mask=sub >= 4)

        diff, keep, inv = [mine(lambda r: spar[n, r]) for n in (0, 4, 3)]

        def forward(i, carry):
            for u in range(4):
                level = i * 4 + u
                flat = pl.ds(pl.multiple_of(level * 8, 8), 8)
                around = jnp.where(
                    top,
                    t[level, a - 1:a + 7] + t[level, a + 1:a + 9],
                    t[level, b - 1:b + 7] + t[level, b + 1:b + 9],
                ) + strip_beside[flat]
                e = (keep * tcentre[level] + diff * around) + carry
                te[level] = e
                carry = mine(lambda r: scoef[level, r]) * e
            return carry

        end = lax.fori_loop(0, HALF // 4, forward, mine(lambda r: spar[2, r]))
        z = mine(lambda r: scoef[HALF, r]) * (te[HALF - 1] + swap_ends(end))
        put(HALF - 1, z * inv)

        def back_level(level, z):
            z = mine(lambda r: scoef[level, r]) * (te[level] + z)
            put(level, z * inv)
            return z

        def back(i, z):
            for u in range(3):
                z = back_level(HALF - 2 - (i * 3 + u), z)
            return z

        back_level(0, lax.fori_loop(0, HALF // 3, back, z))

    copies = []
    for step in range(1, STEPS + 1):
        gather(xs[step - 1], step)
        gather_strip(ts[step - 1], step)
        neighbours()
        if step > 1:
            packages(step - 2, step)
        for f in range(2):
            main_field(xs[step - 1], xs[step], f, step)
            if step < STEPS:
                continue
            for c in range(2):
                copies.append(pltpu.make_async_copy(
                    x4.at[f, :, c, pl.ds(OFF, ROWS)], new_state.at[0, f, :, :, pl.ds(128 * c, 128)], sem.at[f, c]
                ))
                copies[-1].start()
        if step < STEPS:
            strip_step(ts[step - 1], ts[step], step)
    gather(xs[STEPS], STEPS)
    packages(STEPS - 1, STEPS)
    for rt in range(2):
        total = zero
        for q in range(NQ):
            value = []
            for c in range(2):
                got = None
                for n in range(STEPS):
                    stale = sub < n + 1 if rt == 0 else sub >= 7 - n
                    at = q * ROWS + 8 * rt
                    v = jnp.tanh(jnp.where(
                        stale,
                        patch[n, q, c, OFF + 8 * rt:OFF + 8 * rt + 8],
                        sums[n, at:at + 8, 128 * c:128 * c + 128],
                    ))
                    got = v if got is None else got + v
                value.append(got * (1.0 / STEPS))
                mean[q, 8 * rt:8 * rt + 8, 128 * c:128 * c + 128] = value[c]
            ring = jnp.where(lane >= 126, value[1], value[0])
            total = jnp.where((lane >= 4 * q) & (lane < 4 * q + 4), roll(ring, 4 * q + 2), total)
        edges[8 * rt:8 * rt + 8] = total
    for copy in copies:
        copy.wait()


def remap_kernel(table, received, west_edges, east_edges, codes, mask, out):
    lane = lanes()
    for rt in range(2):
        rows = slice(8 * rt, 8 * rt + 8)
        west_edge = west_edges[rows]
        east_edge = east_edges[rows]
        picks, first, second, sea = [], [], [], []
        for c in range(2):
            cols = slice(128 * c, 128 * c + 128)
            code = codes[0, rows, cols]
            offset = code & 3
            row = code >> 2
            w = []
            for j in range(2):
                v = jnp.full((8, 128), table[0, 0, j], F32)
                for n in range(1, 4):
                    v = jnp.where(row == n, table[0, n, j], v)
                w.append(v)
            first.append(w[0])
            second.append(w[1])
            picks.append([offset == n for n in range(1, 4)])
            sea.append(mask[0, rows, cols] == 1)
        for q in range(NQ):
            v = [received[q, rows, 128 * c:128 * c + 128] for c in range(2)]
            shifted = [[None] * 5, [None] * 5]
            for c in range(2):
                shifted[c][2] = v[c]
            for d in (1, 2):
                turned = [roll(u, d) for u in v]
                far = roll(west_edge, d - (4 * q + 2))
                shifted[0][2 - d] = jnp.where(lane < d, far, turned[0])
                shifted[1][2 - d] = jnp.where(lane < d, turned[0], turned[1])
                turned = [roll(u, -d) for u in v]
                far = roll(east_edge, 128 - d - (4 * q + 2))
                shifted[0][2 + d] = jnp.where(lane >= 128 - d, turned[1], turned[0])
                shifted[1][2 + d] = jnp.where(lane >= 128 - d, far, turned[1])
            for c in range(2):
                near, beyond = shifted[c][0], shifted[c][1]
                for n in range(1, 4):
                    near = jnp.where(picks[c][n - 1], shifted[c][n], near)
                    beyond = jnp.where(picks[c][n - 1], shifted[c][n + 1], beyond)
                value = first[c] * near + second[c] * beyond
                out[0, q, rows, 128 * c:128 * c + 128] = jnp.where(sea[c], value, 0.0)


def ring(count, step, periodic):
    pairs = [(i, i + step) for i in range(count)]
    if periodic:
        return [(a, b % count) for a, b in pairs]
    return [(a, b) for a, b in pairs if 0 <= b < count]


FRAME = (2, LEV, 2, TALL, 128)
STRIP = (HALF, TALL, 128)


RIMS = (2 * PLANES + STRIPS // 2, HALO, COLS)
HALVES = (2, 2, HALF * ROWS, COLS)


def load(state, params):
    return pl.pallas_call(
        load_kernel,
        out_shape=(pltpu.VMEM(FRAME, F32), jax.ShapeDtypeStruct((STRIPS, ROWS, 128), F32)),
        in_specs=[HBM, HBM],
        out_specs=[VMEM] * 2,
        scratch_shapes=[
            pltpu.VMEM((3, 2, ROWS, COLS), F32),
            pltpu.SemaphoreType.DMA((4, 2, 2)),
            pltpu.SemaphoreType.DMA,
        ],
        compiler_params=params_of(8),
        name="load",
    )(*[pltpu.with_memory_space_constraint(v, pltpu.HBM) for v in (state, params)])


def prepare(x0, params, couple_weight):
    return pl.pallas_call(
        prepare_kernel,
        out_shape=(
            jax.ShapeDtypeStruct(RIMS, F32),
            jax.ShapeDtypeStruct(RIMS, F32),
            pltpu.VMEM((2, 2, 2 * NQ * ROWS, HALF * ROWS), BF16),
            pltpu.VMEM((2, 2, 2 * NQ * 8, HALF * 8), BF16),
            pltpu.VMEM((2, 2, 3 * COLS, COLS), BF16),
            pltpu.VMEM((256, 128), BF16),
            pltpu.VMEM((5, 2, 2, ROWS, 128), F32),
            pltpu.VMEM((2, HALF + 1, 2, ROWS, 128), F32),
            pltpu.VMEM(HALVES, BF16),
            pltpu.VMEM(HALVES, BF16),
        ),
        in_specs=[VMEM] * 3,
        out_specs=[VMEM] * 10,
        compiler_params=params_of(8),
        name="prepare",
    )(x0, params, couple_weight)


def join(strips, west, east, low_rows, high_rows):
    return pl.pallas_call(
        join_kernel,
        out_shape=(
            jax.ShapeDtypeStruct((STRIPS, ROWS, 128), F32),
            jax.ShapeDtypeStruct(RIMS, F32),
            jax.ShapeDtypeStruct(RIMS, F32),
        ),
        in_specs=[VMEM] * 5,
        out_specs=[VMEM] * 3,
        input_output_aliases={3: 1, 4: 2},
        compiler_params=params_of(8),
        name="join",
    )(strips, west, east, low_rows, high_rows)


def inner(strips, x0, xhi, xlo, par, coef, weights, sides, strip_sides):
    flat = HALF * ROWS
    return pl.pallas_call(
        inner_kernel,
        out_shape=(pltpu.VMEM(FRAME, F32), pltpu.VMEM(HALVES, BF16), pltpu.VMEM(HALVES, BF16))
        + (pltpu.VMEM(FRAME, F32),) * 4
        + (pltpu.VMEM(STRIP, F32),) * 4
        + (pltpu.VMEM((STEPS, NQ * ROWS, COLS), F32),),
        in_specs=[VMEM] * 9,
        out_specs=[VMEM] * 12,
        input_output_aliases={1: 0, 2: 1, 3: 2},
        scratch_shapes=[
            pltpu.VMEM((LEV, 2, ROWS, 128), F32),
            pltpu.VMEM((HALF, ROWS, 128), F32),
            pltpu.VMEM((5, ROWS, 128), F32),
            pltpu.VMEM((HALF + 1, ROWS, 128), F32),
            pltpu.VMEM((flat, 256), BF16),
            pltpu.VMEM((2, 2, flat, COLS), F32),
            pltpu.VMEM((flat, 128), F32),
        ],
        compiler_params=params_of(20),
        name="inner",
    )(strips, x0, xhi, xlo, par, coef, weights, sides, strip_sides)


def outer(*args):
    flat = HALF * 8
    return pl.pallas_call(
        outer_kernel,
        out_shape=(
            jax.ShapeDtypeStruct((1, 2, LEV, ROWS, COLS), F32),
            jax.ShapeDtypeStruct((NQ, ROWS, COLS), F32),
            jax.ShapeDtypeStruct((ROWS, 128), F32),
        ) + (pltpu.VMEM(FRAME, F32),) * 5 + (pltpu.VMEM(STRIP, F32),) * 4,
        in_specs=[VMEM] * 17,
        out_specs=[HBM, VMEM, VMEM] + [VMEM] * 9,
        input_output_aliases={8 + n: 3 + n for n in range(9)},
        scratch_shapes=[
            pltpu.VMEM((LEV, 2, 8, 128), F32),
            pltpu.VMEM((HALF, 8, 128), F32),
            pltpu.VMEM((5, 2, 2, 16, 128), F32),
            pltpu.VMEM((2, HALF + 1, 2, 16, 128), F32),
            pltpu.VMEM((5, 16, 128), F32),
            pltpu.VMEM((HALF + 1, 16, 128), F32),
            pltpu.VMEM((2, LEV, 2, 8, 128), F32),
            pltpu.VMEM((2, 2, flat, COLS), BF16),
            pltpu.VMEM((2, 2, flat, COLS), BF16),
            pltpu.VMEM((HALF, 8, 128), F32),
            pltpu.VMEM((flat, 256), BF16),
            pltpu.VMEM((2, 2, flat, COLS), F32),
            pltpu.VMEM((flat, 128), F32),
            pltpu.VMEM((STEPS, NQ, 2, TALL, 128), F32),
            pltpu.SemaphoreType.DMA((2, 2)),
        ],
        compiler_params=params_of(20),
        name="outer",
    )(*args)


def local(state, params, couple_weight, weight_table, intersection_map, sea_mask):
    lon, lat = lax.axis_size("lon"), lax.axis_size("lat")
    x0, strips = load(state, params)
    west = lax.ppermute(strips, "lon", ring(lon, 1, True))
    east = lax.ppermute(strips, "lon", ring(lon, -1, True))
    low_rows, high_rows, weights, narrow, sides, strip_sides, par, coef, xhi, xlo = prepare(
        x0, params, couple_weight
    )
    strips, low_rows, high_rows = join(strips, west, east, low_rows, high_rows)
    below = lax.ppermute(high_rows, "lat", ring(lat, 1, False))
    above = lax.ppermute(low_rows, "lat", ring(lat, -1, False))
    x0, _, _, *frames, sums = inner(strips, x0, xhi, xlo, par, coef, weights, sides, strip_sides)
    new_state, mean, edges, *_ = outer(
        below, above, strips, params, sums, narrow, sides, strip_sides, x0, *frames
    )
    received = lax.ppermute(mean, "comp", [(0, 1), (1, 0)])

    def across(step):
        return [(a * 2 + s, b * 2 + 1 - s) for a, b in ring(lon, step, True) for s in range(2)]

    west_edges = lax.ppermute(edges, ("lon", "comp"), across(1))
    east_edges = lax.ppermute(edges, ("lon", "comp"), across(-1))
    coupled = pl.pallas_call(
        remap_kernel,
        out_shape=jax.ShapeDtypeStruct((1, NQ, ROWS, COLS), F32),
        in_specs=[SMEM] + [VMEM] * 5,
        out_specs=VMEM,
        compiler_params=params_of(16),
        name="remap",
    )(weight_table, received, west_edges, east_edges, intersection_map, sea_mask)
    return new_state, coupled


def solution(mesh):
    placed = (
        P("comp", None, None, "lat", "lon"),
        P("comp", None, None, "lat", "lon"),
        P("comp", None, None, None),
        P("comp", None, None),
        P("comp", "lat", "lon"),
        P("comp", "lat", "lon"),
    )
    return jax.shard_map(
        local,
        mesh=mesh,
        in_specs=placed,
        out_specs=(P("comp", None, None, "lat", "lon"), P("comp", None, "lat", "lon")),
        check_vma=False,
    )
```

```python
import jax
import jax.numpy as jnp
from jax import lax
from jax.experimental import pallas as pl
from jax.experimental.pallas import tpu as pltpu
from jax.sharding import PartitionSpec as P

STEPS = 4
LEV = 64
HALF = LEV // 2
ROWS = 16
HALO = 4
COLS = 256
NQ = 8
OFF = 8
TALL = 32
PLANES = LEV + 3
STRIPS = HALF // 2 + 2
VMEM = pl.BlockSpec(memory_space=pltpu.VMEM)
SMEM = pl.BlockSpec(memory_space=pltpu.SMEM)
HBM = pl.BlockSpec(memory_space=pltpu.HBM)
BF16 = jnp.bfloat16
F32 = jnp.float32


def lanes():
    return lax.broadcasted_iota(jnp.int32, (8, 128), 1)


def subs():
    return lax.broadcasted_iota(jnp.int32, (8, 128), 0)


def level_of(level, h):
    return level if h == 0 else LEV - 1 - level


def halves(value):
    high = value.astype(BF16)
    return high, (value - high.astype(F32)).astype(BF16)


def params_of(vmem):
    return pltpu.CompilerParams(vmem_limit_bytes=vmem * 2**20)


def roll(value, shift):
    return pltpu.roll(value, shift % 128, 1)


def load_kernel(state, params, x0, strips, near, sem, near_sem):
    lane = lanes()
    part = LEV // 4
    copies = {}
    for n in (0, 3, 1, 2):
        for f in range(2):
            for c in range(2):
                copies[n, f, c] = pltpu.make_async_copy(
                    state.at[0, f, pl.ds(part * n, part), :, pl.ds(128 * c, 128)],
                    x0.at[f, pl.ds(part * n, part), c, pl.ds(OFF, ROWS)],
                    sem.at[n, f, c],
                )
                copies[n, f, c].start()
    small = pltpu.make_async_copy(params.at[0], near, near_sem)
    small.start()

    def place(total, source, index):
        ring = jnp.where(lane >= 124, source[1], source[0])
        first = roll(ring, 16 * index + 4)
        second = roll(ring, 16 * index + 12)
        inside = (lane >= 16 * index) & (lane < 16 * index + 16)
        pair = jnp.where((lane & 8) == 0, first, second)
        return pair if total is None else jnp.where(inside, pair, total)

    def strip(i, carry):
        made = []
        for block in (i * 2, i * 2 + 1):
            for rt in range(2):
                at = OFF + 8 * rt
                total = None
                for lq in range(2):
                    for f in range(2):
                        for h in range(2):
                            lam = level_of(block * 2 + lq, h)
                            source = [x0[f, lam, c, at:at + 8] for c in range(2)]
                            total = place(total, source, lq * 4 + f * 2 + h)
                made.append((block, rt, total))
        for block, rt, total in made:
            strips[block, 8 * rt:8 * rt + 8] = total
        return carry

    for n in range(2):
        for m in (n, 3 - n):
            for f in range(2):
                for c in range(2):
                    copies[m, f, c].wait()
        lax.fori_loop(n * part // 4, (n + 1) * part // 4, strip, 0)
    small.wait()
    for rt in range(2):
        rows = slice(8 * rt, 8 * rt + 8)
        total = None
        for lq in range(2):
            for f in range(2):
                for h in range(2):
                    source = [near[lq, f, rows, 128 * c:128 * c + 128] for c in range(2)]
                    total = place(total, source, lq * 4 + f * 2 + h)
        strips[HALF // 2, rows] = total
        total = jnp.zeros((8, 128), F32)
        for f in range(2):
            source = [near[2, f, rows, 128 * c:128 * c + 128] for c in range(2)]
            total = place(total, source, f * 2)
        strips[HALF // 2 + 1, rows] = total


def join_kernel(strips, west, east, low_in, high_in, joined, low_rows, high_rows):
    place = lanes() & 15
    for block in range(STRIPS):
        for rt in range(2):
            rows = slice(8 * rt, 8 * rt + 8)
            joined[block, rows] = jnp.where(
                place < 4, west[block, rows], jnp.where(place >= 12, east[block, rows], strips[block, rows])
            )
        cols = slice(128 * (block % 2), 128 * (block % 2) + 128)
        low_rows[2 * PLANES + block // 2, :, cols] = joined[block, 0:HALO]
        high_rows[2 * PLANES + block // 2, :, cols] = joined[block, ROWS - HALO:ROWS]


def kron_weights(couple_weight, out, rows):
    width = HALF * rows
    level = lax.broadcasted_iota(jnp.int32, (LEV, width), 0)
    place = lax.broadcasted_iota(jnp.int32, (LEV, width), 1)
    spread = []
    for h in range(2):
        first = rows * level_of(level, h)
        spread.append(((place >= first) & (place < first + rows)).astype(F32).astype(BF16))
    row = lax.broadcasted_iota(jnp.int32, (rows, width), 0)
    within = lax.broadcasted_iota(jnp.int32, (rows, width), 1) & (rows - 1)
    keep = within == row
    for f in range(2):
        for n, part in enumerate(halves(couple_weight[0, :, f, :])):
            for h in range(2):
                wide = jnp.dot(part, spread[h], preferred_element_type=F32)
                for q in range(0, NQ, 2):
                    at = n * NQ * rows + q * rows
                    pair = [jnp.where(keep, wide[q + i:q + i + 1], 0.0) for i in range(2)]
                    out[f, h, at:at + 2 * rows] = jnp.concatenate(pair, axis=0).astype(BF16)


def prepare_kernel(x0, params, couple_weight,
                   low_rows, high_rows, weights, narrow, sides, strip_sides, par, coef, xhi, xlo):
    def some(level, carry):
        at = pl.ds(pl.multiple_of(level * ROWS, 16), ROWS)
        for f in range(2):
            for h in range(2):
                lam = level_of(level, h)
                for c in range(2):
                    cols = slice(128 * c, 128 * c + 128)
                    value = x0[f, lam, c, OFF:OFF + ROWS]
                    high, low = halves(value)
                    xhi[f, h, at, cols] = high
                    xlo[f, h, at, cols] = low
                    low_rows[f * PLANES + lam, :, cols] = x0[f, lam, c, OFF:OFF + HALO]
                    high_rows[f * PLANES + lam, :, cols] = x0[f, lam, c, OFF + ROWS - HALO:OFF + ROWS]
        return carry

    for f in range(2):
        for kind in range(3):
            low_rows[f * PLANES + LEV + kind] = params[0, kind, f, 0:HALO]
            high_rows[f * PLANES + LEV + kind] = params[0, kind, f, ROWS - HALO:ROWS]
    columns = [(f, c, rt) for f in range(2) for c in range(2) for rt in range(2)]
    for f, c, rt in columns:
        rows = slice(8 * rt, 8 * rt + 8)
        h, k, g = [params[0, kind, f, rows, 128 * c:128 * c + 128] for kind in range(3)]
        for n, value in enumerate((h, k, g, 1.0 / k, 1.0 - 4.0 * h)):
            par[n, f, c, rows] = value

    def pivots(i, carry):
        out = []
        for n, (f, c, rt) in enumerate(columns):
            rows = slice(8 * rt, 8 * rt + 8)
            out.append(pivot_levels(coef, (f,), (c, rows), q[n], carry[n], i * 2, 2))
        for u in range(2):
            some(i * 2 + u, 0)
        return tuple(out)

    q = [ratio(par[1, f, c, 8 * rt:8 * rt + 8]) for f, c, rt in columns]
    lax.fori_loop(0, HALF // 2, pivots, tuple(q))
    for f, c, rt in columns:
        rows = slice(8 * rt, 8 * rt + 8)
        m = coef[f, HALF - 1, c, rows]
        coef[f, HALF, c, rows] = m / (1.0 - m * m)
    kron_weights(couple_weight, weights, ROWS)
    kron_weights(couple_weight, narrow, 8)
    row = lax.broadcasted_iota(jnp.int32, (COLS, COLS), 0)
    col = lax.broadcasted_iota(jnp.int32, (COLS, COLS), 1)
    inner = (jnp.abs(row - col) == 1).astype(F32).astype(jnp.bfloat16)
    lane = row & 127
    for f in range(2):
        for h in range(2):
            base = f * 32 + h * 16
            rim = ((lane == base + 3) & (col == 0)) | ((lane == base + 12) & (col == COLS - 1))
            sides[f, h, 0:COLS] = inner
            sides[f, h, COLS:2 * COLS] = inner
            sides[f, h, 2 * COLS:3 * COLS] = rim.astype(F32).astype(jnp.bfloat16)
    near = jnp.abs((row & 127) - col)[:, 0:128] == 1
    strip_sides[...] = near.astype(F32).astype(jnp.bfloat16)

def ratio(k):
    root = jnp.sqrt(1.0 + 4.0 * k) + 1.0
    return 4.0 * k / (root * root)


def pivot_levels(ref, index, rows, q, power, first, count):
    square = q * q
    for u in range(count):
        above = power * square
        ref[*index, first + u, *rows] = q * (1.0 + power) / (1.0 + above)
        power = above
    return power


def strip_params(spar):
    for rt in range(2):
        rows = slice(8 * rt, 8 * rt + 8)
        k = spar[1, rows]
        k = jnp.where(k > 0.0, k, 1.0)
        spar[5, rows] = ratio(k)
        spar[3, rows] = 1.0 / k
        spar[4, rows] = 1.0 - 4.0 * spar[0, rows]


def strip_pivots(spar, scoef, first, count, carry):
    out = []
    for rt in range(2):
        rows = slice(8 * rt, 8 * rt + 8)
        out.append(pivot_levels(scoef, (), (rows,), spar[5, rows], carry[rt], first, count))
    return tuple(out)


def strip_closing(scoef):
    for rt in range(2):
        rows = slice(8 * rt, 8 * rt + 8)
        m = scoef[HALF - 1, rows]
        scoef[HALF, rows] = m / (1.0 - m * m)


def swap_ends(value):
    return jnp.where((lanes() & 16) == 0, roll(value, -16), roll(value, 16))


def inner_kernel(strips, x0_in, xhi_in, xlo_in, par, coef, weights, narrow, sides, strip_sides,
                 x0, xhi, xlo, x1, x2, x3, x4, t0, t1, t2, t3, sums, middle,
                 xe, te, spar, scoef, tsplit, beside, strip_beside):
    xs, ts = (x0, x1, x2, x3, x4), (t0, t1, t2, t3)
    sub = subs()
    zero = jnp.zeros((8, 128), F32)

    for rt in range(2):
        rows = slice(8 * rt, 8 * rt + 8)
        spar[0, rows] = strips[HALF // 2, rows]
        spar[1, rows] = roll(strips[HALF // 2, rows], 64)
        spar[2, rows] = strips[HALF // 2 + 1, rows]
    strip_params(spar)

    def unstrip(i, carry):
        levels = []
        for u in range(4):
            block = i * 4 + u
            for lq in range(2):
                tiles = [roll(strips[block, 8 * rt:8 * rt + 8], 64 * lq) for rt in range(2)]
                levels.append((block * 2 + lq, tiles))
        for level, tiles in levels:
            for rt in range(2):
                t0[level, OFF + 8 * rt:OFF + 8 * rt + 8] = tiles[rt]
            split_strip(level, tiles)
        return strip_pivots(spar, scoef, i * 8, 8, carry)

    def split_strip(level, tiles):
        at = pl.ds(pl.multiple_of(level * ROWS, 16), ROWS)
        high, low = halves(jnp.concatenate(tiles, axis=0))
        tsplit[at, 0:128] = high
        tsplit[at, 128:256] = low

    lax.fori_loop(0, HALF // 8, unstrip, (spar[5, 0:8], spar[5, 8:16]))
    strip_closing(scoef)

    def vertical(load, rt):
        at = OFF + 8 * rt
        up, down = load(at - 1), load(at + 1)
        if rt == 0:
            up = jnp.where(sub == 0, 0.0, up)
        else:
            down = jnp.where(sub == 7, 0.0, down)
        return up + down

    def neighbours():
        def part(i, carry):
            at = pl.ds(pl.multiple_of(i * 256, 16), 256)
            for f in range(2):
                for h in range(2):
                    value = jnp.concatenate([xhi[f, h, at], xlo[f, h, at], tsplit[at]], axis=1)
                    beside[f, h, at] = jnp.dot(value, sides[f, h], preferred_element_type=F32)
            strip_beside[at] = jnp.dot(tsplit[at], strip_sides[...], preferred_element_type=F32)
            return carry

        lax.fori_loop(0, HALF * ROWS // 256, part, 0)

    def packages(n):
        total = None
        for f in range(2):
            for h in range(2):
                both = jnp.dot(weights[f, h], xhi[f, h], preferred_element_type=F32)
                high = jnp.dot(weights[f, h, :NQ * ROWS], xlo[f, h], preferred_element_type=F32)
                value = (both[NQ * ROWS:] + high) + both[:NQ * ROWS]
                total = value if total is None else total + value
        sums[n] = total

    def main_field(x, xn, f, halve):
        tiles = [(c, rt, slice(8 * rt, 8 * rt + 8), OFF + 8 * rt) for c in range(2) for rt in range(2)]
        diff = [par[0, f, c, rows] for c, rt, rows, at in tiles]
        keep = [par[4, f, c, rows] for c, rt, rows, at in tiles]

        def forward(i, carry):
            carry = list(carry)
            for u in range(4):
                level = i * 4 + u
                for n, (c, rt, rows, at) in enumerate(tiles):
                    m = coef[f, level, c, rows]
                    flat = pl.ds(pl.multiple_of(level * ROWS, 8) + 8 * rt, 8)
                    for h in range(2):
                        lam = level_of(level, h)
                        around = vertical(lambda r: x[f, lam, c, r:r + 8], rt)
                        around = around + beside[f, h, flat, 128 * c:128 * c + 128]
                        e = (keep[n] * x[f, lam, c, at:at + 8] + diff[n] * around) + carry[h * 4 + n]
                        xe[lam, c, rows] = e
                        carry[h * 4 + n] = m * e
            return tuple(carry)

        start = tuple(par[2, f, c, rows] for c, rt, rows, at in tiles) + (zero,) * 4
        ends = lax.fori_loop(0, HALF // 4, forward, start)
        inv = [par[3, f, c, rows] for c, rt, rows, at in tiles]

        def finish(level, h, z):
            lam = level_of(level, h)
            flat = pl.ds(pl.multiple_of(level * ROWS, 16), ROWS)
            for c in range(2):
                y = []
                for rt in range(2):
                    v = z[h * 4 + 2 * c + rt] * inv[2 * c + rt]
                    xn[f, lam, c, OFF + 8 * rt:OFF + 8 * rt + 8] = v
                    y.append(v)
                if not halve:
                    continue
                high, low = halves(jnp.concatenate(y, axis=0))
                xhi[f, h, flat, 128 * c:128 * c + 128] = high
                xlo[f, h, flat, 128 * c:128 * c + 128] = low

        z = [None] * 8
        for h in range(2):
            for n, (c, rt, rows, at) in enumerate(tiles):
                z[h * 4 + n] = coef[f, HALF, c, rows] * (xe[HALF - 1 + h, c, rows] + ends[(1 - h) * 4 + n])
        for h in range(2):
            finish(HALF - 1, h, z)

        def back_level(level, z):
            out = [None] * 8
            for h in range(2):
                lam = level_of(level, h)
                for n, (c, rt, rows, at) in enumerate(tiles):
                    out[h * 4 + n] = coef[f, level, c, rows] * (xe[lam, c, rows] + z[h * 4 + n])
                finish(level, h, out)
            return tuple(out)

        def back(i, z):
            for u in range(3):
                z = back_level(HALF - 2 - (i * 3 + u), z)
            return z

        z = lax.fori_loop(0, HALF // 3, back, tuple(z))
        back_level(0, z)

    def strip_step(t, tn):
        tiles = [slice(8 * rt, 8 * rt + 8) for rt in range(2)]
        diff = [spar[0, rows] for rows in tiles]
        inv = [spar[3, rows] for rows in tiles]
        keep = [spar[4, rows] for rows in tiles]

        def forward(i, carry):
            carry = list(carry)
            for u in range(4):
                level = i * 4 + u
                for rt, rows in enumerate(tiles):
                    flat = pl.ds(pl.multiple_of(level * ROWS, 8) + 8 * rt, 8)
                    around = vertical(lambda r: t[level, r:r + 8], rt) + strip_beside[flat]
                    e = (keep[rt] * t[level, OFF + 8 * rt:OFF + 8 * rt + 8] + diff[rt] * around) + carry[rt]
                    te[level, rows] = e
                    carry[rt] = scoef[level, rows] * e
            return tuple(carry)

        ends = lax.fori_loop(0, HALF // 4, forward, tuple(spar[2, rows] for rows in tiles))
        def finish(level, z):
            y = [z[rt] * inv[rt] for rt in range(2)]
            for rt in range(2):
                tn[level, OFF + 8 * rt:OFF + 8 * rt + 8] = y[rt]
            split_strip(level, y)

        z = [scoef[HALF, rows] * (te[HALF - 1, rows] + swap_ends(ends[rt])) for rt, rows in enumerate(tiles)]
        finish(HALF - 1, z)

        def back_level(level, z):
            out = [scoef[level, rows] * (te[level, rows] + z[rt]) for rt, rows in enumerate(tiles)]
            finish(level, out)
            return tuple(out)

        def back(i, z):
            for u in range(3):
                z = back_level(HALF - 2 - (i * 3 + u), z)
            return z

        z = lax.fori_loop(0, HALF // 3, back, tuple(z))
        back_level(0, z)

    begin, rows8 = OFF + 4, slice(4, 12)

    def halve_middle(x, t):
        def some(i, carry):
            at = pl.ds(pl.multiple_of(i * 16, 16), 16)
            for f in range(2):
                for h in range(2):
                    for c in range(2):
                        pair = [x[f, level_of(i * 2 + u, h), c, begin:begin + 8] for u in range(2)]
                        high, low = halves(jnp.concatenate(pair, axis=0))
                        xhi[f, h, at, 128 * c:128 * c + 128] = high
                        xlo[f, h, at, 128 * c:128 * c + 128] = low
            if t is not None:
                pair = [t[i * 2 + u, begin:begin + 8] for u in range(2)]
                high, low = halves(jnp.concatenate(pair, axis=0))
                tsplit[at, 0:128] = high
                tsplit[at, 128:256] = low
            return carry

        lax.fori_loop(0, HALF // 2, some, 0)

    def neighbours_middle():
        for f in range(2):
            for h in range(2):
                value = jnp.concatenate([xhi[f, h, 0:256], xlo[f, h, 0:256], tsplit[0:256]], axis=1)
                beside[f, h, 0:256] = jnp.dot(value, sides[f, h], preferred_element_type=F32)

    def packages_middle(n):
        total = None
        for f in range(2):
            for h in range(2):
                both = jnp.dot(narrow[f, h], xhi[f, h, 0:256], preferred_element_type=F32)
                high = jnp.dot(narrow[f, h, :NQ * 8], xlo[f, h, 0:256], preferred_element_type=F32)
                value = (both[NQ * 8:] + high) + both[:NQ * 8]
                total = value if total is None else total + value
        middle[n, 8:8 + NQ * 8] = total

    def main_middle(x, xn, f):
        diff = [par[0, f, c, rows8] for c in range(2)]
        keep = [par[4, f, c, rows8] for c in range(2)]
        inv = [par[3, f, c, rows8] for c in range(2)]

        def forward(i, carry):
            carry = list(carry)
            for u in range(8):
                level = i * 8 + u
                flat = pl.ds(pl.multiple_of(level * 8, 8), 8)
                for c in range(2):
                    m = coef[f, level, c, rows8]
                    for h in range(2):
                        lam = level_of(level, h)
                        around = x[f, lam, c, begin - 1:begin + 7] + x[f, lam, c, begin + 1:begin + 9]
                        around = around + beside[f, h, flat, 128 * c:128 * c + 128]
                        e = (keep[c] * x[f, lam, c, begin:begin + 8] + diff[c] * around) + carry[h * 2 + c]
                        xe[lam, c, 0:8] = e
                        carry[h * 2 + c] = m * e
            return tuple(carry)

        start = (par[2, f, 0, rows8], par[2, f, 1, rows8], zero, zero)
        ends = lax.fori_loop(0, HALF // 8, forward, start)
        z = []
        for h in range(2):
            for c in range(2):
                v = coef[f, HALF, c, rows8] * (xe[HALF - 1 + h, c, 0:8] + ends[(1 - h) * 2 + c])
                xn[f, HALF - 1 + h, c, begin:begin + 8] = v * inv[c]
                z.append(v)

        def back_level(level, z):
            out = [None] * 4
            for c in range(2):
                m = coef[f, level, c, rows8]
                for h in range(2):
                    lam = level_of(level, h)
                    v = m * (xe[lam, c, 0:8] + z[h * 2 + c])
                    xn[f, lam, c, begin:begin + 8] = v * inv[c]
                    out[h * 2 + c] = v
            return tuple(out)

        def back(i, z):
            for u in range(10):
                z = back_level(HALF - 2 - (i * 10 + u), z)
            return z

        z = lax.fori_loop(0, HALF // 10, back, tuple(z))
        back_level(0, z)

    for step in range(STEPS - 1):
        neighbours()
        if step > 0:
            packages(step - 1)
        for f in range(2):
            main_field(xs[step], xs[step + 1], f, step < STEPS - 2)
        strip_step(ts[step], ts[step + 1])
    halve_middle(x3, t3)
    neighbours_middle()
    packages_middle(0)
    for f in range(2):
        main_middle(x3, x4, f)
    halve_middle(x4, None)
    packages_middle(1)


def outer_kernel(below, above, strips, params, sums, middle, narrow, sides, strip_sides,
                 i0, i1, i2, i3, i4, j0, j1, j2, j3,
                 new_state, mean, edges, x0, x1, x2, x3, x4, t0, t1, t2, t3,
                 xe, te, par, coef, spar, scoef, centre, xhi, xlo, tcentre, tsplit, beside, strip_beside, patch, sem):
    xs, ts = (x0, x1, x2, x3, x4), (t0, t1, t2, t3)
    lane, sub = lanes(), subs()
    top = sub < 4
    zero = jnp.zeros((8, 128), F32)

    def strip_rim(ref, block):
        return ref[2 * PLANES + block // 2, :, 128 * (block % 2):128 * (block % 2) + 128]

    for n, (block, shift) in enumerate(((HALF // 2, 0), (HALF // 2, 64), (HALF // 2 + 1, 0))):
        spar[n, 0:4] = pltpu.roll(strip_rim(below, block), shift, 1)
        spar[n, 4:8] = pltpu.roll(strips[block, 0:4], shift, 1)
        spar[n, 8:12] = pltpu.roll(strips[block, 12:16], shift, 1)
        spar[n, 12:16] = pltpu.roll(strip_rim(above, block), shift, 1)
    strip_params(spar)
    columns = [(f, c, rt) for f in range(2) for c in range(2) for rt in range(2)]
    for f in range(2):
        for c in range(2):
            cols = slice(128 * c, 128 * c + 128)
            for n in range(3):
                par[n, f, c, 0:4] = below[f * PLANES + LEV + n, :, cols]
                par[n, f, c, 4:8] = params[0, n, f, 0:4, cols]
                par[n, f, c, 8:12] = params[0, n, f, 12:16, cols]
                par[n, f, c, 12:16] = above[f * PLANES + LEV + n, :, cols]
    for f, c, rt in columns:
        rows = slice(8 * rt, 8 * rt + 8)
        k = par[1, f, c, rows]
        k = jnp.where(k > 0.0, k, 1.0)
        par[5, f, c, rows] = ratio(k)
        par[3, f, c, rows] = 1.0 / k
        par[4, f, c, rows] = 1.0 - 4.0 * par[0, f, c, rows]

    def pivots(i, carry):
        out = []
        for n, (f, c, rt) in enumerate(columns):
            rows = slice(8 * rt, 8 * rt + 8)
            out.append(pivot_levels(coef, (f,), (c, rows), par[5, f, c, rows], carry[n], i * 4, 4))
        out.extend(strip_pivots(spar, scoef, i * 4, 4, carry[len(columns):]))
        for u in range(4):
            for f in range(2):
                for h in range(2):
                    lam = level_of(i * 4 + u, h)
                    for c in range(2):
                        cols = slice(128 * c, 128 * c + 128)
                        x0[f, lam, c, OFF - HALO:OFF] = below[f * PLANES + lam, :, cols]
                        x0[f, lam, c, OFF + ROWS:OFF + ROWS + HALO] = above[f * PLANES + lam, :, cols]
        rims = []
        for c in range(2):
            cols = slice(128 * c, 128 * c + 128)
            for lq in range(2):
                rims.append(pltpu.roll(below[2 * PLANES + i, :, cols], 64 * lq, 1))
                rims.append(pltpu.roll(above[2 * PLANES + i, :, cols], 64 * lq, 1))
        for n in range(4):
            t0[i * 4 + n, OFF - HALO:OFF] = rims[2 * n]
            t0[i * 4 + n, OFF + ROWS:OFF + ROWS + HALO] = rims[2 * n + 1]
        return tuple(out)

    start = [par[5, f, c, 8 * rt:8 * rt + 8] for f, c, rt in columns] + [spar[5, 0:8], spar[5, 8:16]]
    lax.fori_loop(0, HALF // 4, pivots, tuple(start))
    for f, c, rt in columns:
        rows = slice(8 * rt, 8 * rt + 8)
        m = coef[f, HALF - 1, c, rows]
        coef[f, HALF, c, rows] = m / (1.0 - m * m)
    strip_closing(scoef)

    def gather(x, step):
        a, b = OFF - 4 + step, OFF + 12 - step

        def some(i, carry):
            at = pl.ds(pl.multiple_of(i * 16, 16), 16)
            for f in range(2):
                for h in range(2):
                    for c in range(2):
                        pair = []
                        for u in range(2):
                            lam = level_of(i * 2 + u, h)
                            v = jnp.where(top, x[f, lam, c, a:a + 8], x[f, lam, c, b:b + 8])
                            centre[f, lam, c] = v
                            pair.append(v)
                        high, low = halves(jnp.concatenate(pair, axis=0))
                        xhi[f, h, at, 128 * c:128 * c + 128] = high
                        xlo[f, h, at, 128 * c:128 * c + 128] = low
            return carry

        lax.fori_loop(0, HALF // 2, some, 0)

    def gather_strip(t, step):
        a, b = OFF - 4 + step, OFF + 12 - step

        def some(i, carry):
            at = pl.ds(pl.multiple_of(i * 16, 16), 16)
            pair = []
            for u in range(2):
                v = jnp.where(top, t[i * 2 + u, a:a + 8], t[i * 2 + u, b:b + 8])
                tcentre[i * 2 + u] = v
                pair.append(v)
            high, low = halves(jnp.concatenate(pair, axis=0))
            tsplit[at, 0:128] = high
            tsplit[at, 128:256] = low
            return carry

        lax.fori_loop(0, HALF // 2, some, 0)

    def neighbours():
        for f in range(2):
            for h in range(2):
                value = jnp.concatenate([xhi[f, h], xlo[f, h], tsplit[...]], axis=1)
                beside[f, h] = jnp.dot(value, sides[f, h], preferred_element_type=F32)
        strip_beside[...] = jnp.dot(tsplit[...], strip_sides[...], preferred_element_type=F32)

    def packages(n, step):
        a, b = OFF - 4 + step, OFF + 12 - step
        total = None
        for f in range(2):
            for h in range(2):
                both = jnp.dot(narrow[f, h], xhi[f, h], preferred_element_type=F32)
                high = jnp.dot(narrow[f, h, :NQ * 8], xlo[f, h], preferred_element_type=F32)
                value = (both[NQ * 8:] + high) + both[:NQ * 8]
                total = value if total is None else total + value
        for q in range(NQ):
            for c in range(2):
                v = total[q * 8:q * 8 + 8, 128 * c:128 * c + 128]
                pltpu.store(patch.at[n, q, c, pl.ds(a, 8)], v, mask=top)
                pltpu.store(patch.at[n, q, c, pl.ds(b, 8)], v, mask=sub >= 4)

    def main_field(x, xn, f, step):
        a, b = OFF - 4 + step, OFF + 12 - step

        def mine(load):
            return jnp.where(top, load(slice(step, step + 8)), load(slice(8 - step, 16 - step)))

        def put(lam, c, v):
            pltpu.store(xn.at[f, lam, c, pl.ds(a, 8)], v, mask=top)
            pltpu.store(xn.at[f, lam, c, pl.ds(b, 8)], v, mask=sub >= 4)

        diff = [mine(lambda r: par[0, f, c, r]) for c in range(2)]
        keep = [mine(lambda r: par[4, f, c, r]) for c in range(2)]
        inv = [mine(lambda r: par[3, f, c, r]) for c in range(2)]

        def forward(i, carry):
            carry = list(carry)
            for u in range(4):
                level = i * 4 + u
                m = [mine(lambda r: coef[f, level, c, r]) for c in range(2)]
                flat = pl.ds(pl.multiple_of(level * 8, 8), 8)
                for h in range(2):
                    lam = level_of(level, h)
                    for c in range(2):
                        around = jnp.where(
                            top,
                            x[f, lam, c, a - 1:a + 7] + x[f, lam, c, a + 1:a + 9],
                            x[f, lam, c, b - 1:b + 7] + x[f, lam, c, b + 1:b + 9],
                        ) + beside[f, h, flat, 128 * c:128 * c + 128]
                        e = (keep[c] * centre[f, lam, c] + diff[c] * around) + carry[h * 2 + c]
                        xe[lam, c] = e
                        carry[h * 2 + c] = m[c] * e
            return tuple(carry)

        start = (mine(lambda r: par[2, f, 0, r]), mine(lambda r: par[2, f, 1, r]), zero, zero)
        ends = lax.fori_loop(0, HALF // 4, forward, start)
        z = []
        for h in range(2):
            for c in range(2):
                v = mine(lambda r: coef[f, HALF, c, r]) * (xe[HALF - 1 + h, c] + ends[(1 - h) * 2 + c])
                put(HALF - 1 + h, c, v * inv[c])
                z.append(v)

        def back_level(level, z):
            out = []
            m = [mine(lambda r: coef[f, level, c, r]) for c in range(2)]
            for h in range(2):
                lam = level_of(level, h)
                for c in range(2):
                    v = m[c] * (xe[lam, c] + z[h * 2 + c])
                    put(lam, c, v * inv[c])
                    out.append(v)
            return tuple(out)

        def back(i, z):
            for u in range(10):
                z = back_level(HALF - 2 - (i * 10 + u), z)
            return z

        z = lax.fori_loop(0, HALF // 10, back, tuple(z))
        back_level(0, z)

    def strip_step(t, tn, step):
        a, b = OFF - 4 + step, OFF + 12 - step

        def mine(load):
            return jnp.where(top, load(slice(step, step + 8)), load(slice(8 - step, 16 - step)))

        def put(level, v):
            pltpu.store(tn.at[level, pl.ds(a, 8)], v, mask=top)
            pltpu.store(tn.at[level, pl.ds(b, 8)], v, mask=sub >= 4)

        diff, keep, inv = [mine(lambda r: spar[n, r]) for n in (0, 4, 3)]

        def forward(i, carry):
            for u in range(4):
                level = i * 4 + u
                flat = pl.ds(pl.multiple_of(level * 8, 8), 8)
                around = jnp.where(
                    top,
                    t[level, a - 1:a + 7] + t[level, a + 1:a + 9],
                    t[level, b - 1:b + 7] + t[level, b + 1:b + 9],
                ) + strip_beside[flat]
                e = (keep * tcentre[level] + diff * around) + carry
                te[level] = e
                carry = mine(lambda r: scoef[level, r]) * e
            return carry

        end = lax.fori_loop(0, HALF // 4, forward, mine(lambda r: spar[2, r]))
        z = mine(lambda r: scoef[HALF, r]) * (te[HALF - 1] + swap_ends(end))
        put(HALF - 1, z * inv)

        def back_level(level, z):
            z = mine(lambda r: scoef[level, r]) * (te[level] + z)
            put(level, z * inv)
            return z

        def back(i, z):
            for u in range(3):
                z = back_level(HALF - 2 - (i * 3 + u), z)
            return z

        back_level(0, lax.fori_loop(0, HALF // 3, back, z))

    copies = []
    for step in range(1, STEPS + 1):
        gather(xs[step - 1], step)
        gather_strip(ts[step - 1], step)
        neighbours()
        if step > 1:
            packages(step - 2, step)
        for f in range(2):
            main_field(xs[step - 1], xs[step], f, step)
            if step < STEPS:
                continue
            for c in range(2):
                copies.append(pltpu.make_async_copy(
                    x4.at[f, :, c, pl.ds(OFF, ROWS)], new_state.at[0, f, :, :, pl.ds(128 * c, 128)], sem.at[f, c]
                ))
                copies[-1].start()
        if step < STEPS:
            strip_step(ts[step - 1], ts[step], step)
    gather(xs[STEPS], STEPS)
    packages(STEPS - 1, STEPS)
    for rt in range(2):
        total = zero
        for q in range(NQ):
            value = []
            for c in range(2):
                got = None
                for n in range(STEPS):
                    cols = slice(128 * c, 128 * c + 128)
                    if n < 2:
                        stale = sub < n + 1 if rt == 0 else sub >= 7 - n
                        own = sums[n, q * ROWS + 8 * rt:q * ROWS + 8 * rt + 8, cols]
                    else:
                        stale = top if rt == 0 else sub >= 4
                        own = middle[n - 2, 4 + 8 * q + 8 * rt:12 + 8 * q + 8 * rt, cols]
                    v = jnp.tanh(jnp.where(stale, patch[n, q, c, OFF + 8 * rt:OFF + 8 * rt + 8], own))
                    got = v if got is None else got + v
                value.append(got * (1.0 / STEPS))
                mean[q, 8 * rt:8 * rt + 8, 128 * c:128 * c + 128] = value[c]
            ring = jnp.where(lane >= 126, value[1], value[0])
            total = jnp.where((lane >= 4 * q) & (lane < 4 * q + 4), roll(ring, 4 * q + 2), total)
        edges[8 * rt:8 * rt + 8] = total
    for copy in copies:
        copy.wait()


def remap_kernel(table, received, west_edges, east_edges, codes, mask, out):
    lane = lanes()
    for rt in range(2):
        rows = slice(8 * rt, 8 * rt + 8)
        west_edge = west_edges[rows]
        east_edge = east_edges[rows]
        picks, first, second, sea = [], [], [], []
        for c in range(2):
            cols = slice(128 * c, 128 * c + 128)
            code = codes[0, rows, cols]
            offset = code & 3
            row = code >> 2
            w = []
            for j in range(2):
                v = jnp.full((8, 128), table[0, 0, j], F32)
                for n in range(1, 4):
                    v = jnp.where(row == n, table[0, n, j], v)
                w.append(v)
            first.append(w[0])
            second.append(w[1])
            picks.append([offset == n for n in range(1, 4)])
            sea.append(mask[0, rows, cols] == 1)
        for q in range(NQ):
            v = [received[q, rows, 128 * c:128 * c + 128] for c in range(2)]
            shifted = [[None] * 5, [None] * 5]
            for c in range(2):
                shifted[c][2] = v[c]
            for d in (1, 2):
                turned = [roll(u, d) for u in v]
                far = roll(west_edge, d - (4 * q + 2))
                shifted[0][2 - d] = jnp.where(lane < d, far, turned[0])
                shifted[1][2 - d] = jnp.where(lane < d, turned[0], turned[1])
                turned = [roll(u, -d) for u in v]
                far = roll(east_edge, 128 - d - (4 * q + 2))
                shifted[0][2 + d] = jnp.where(lane >= 128 - d, turned[1], turned[0])
                shifted[1][2 + d] = jnp.where(lane >= 128 - d, far, turned[1])
            for c in range(2):
                near, beyond = shifted[c][0], shifted[c][1]
                for n in range(1, 4):
                    near = jnp.where(picks[c][n - 1], shifted[c][n], near)
                    beyond = jnp.where(picks[c][n - 1], shifted[c][n + 1], beyond)
                value = first[c] * near + second[c] * beyond
                out[0, q, rows, 128 * c:128 * c + 128] = jnp.where(sea[c], value, 0.0)


def ring(count, step, periodic):
    pairs = [(i, i + step) for i in range(count)]
    if periodic:
        return [(a, b % count) for a, b in pairs]
    return [(a, b) for a, b in pairs if 0 <= b < count]


FRAME = (2, LEV, 2, TALL, 128)
STRIP = (HALF, TALL, 128)


RIMS = (2 * PLANES + STRIPS // 2, HALO, COLS)
HALVES = (2, 2, HALF * ROWS, COLS)


def load(state, params):
    return pl.pallas_call(
        load_kernel,
        out_shape=(pltpu.VMEM(FRAME, F32), jax.ShapeDtypeStruct((STRIPS, ROWS, 128), F32)),
        in_specs=[HBM, HBM],
        out_specs=[VMEM] * 2,
        scratch_shapes=[
            pltpu.VMEM((3, 2, ROWS, COLS), F32),
            pltpu.SemaphoreType.DMA((4, 2, 2)),
            pltpu.SemaphoreType.DMA,
        ],
        compiler_params=params_of(8),
        name="load",
    )(*[pltpu.with_memory_space_constraint(v, pltpu.HBM) for v in (state, params)])


def prepare(x0, params, couple_weight):
    return pl.pallas_call(
        prepare_kernel,
        out_shape=(
            jax.ShapeDtypeStruct(RIMS, F32),
            jax.ShapeDtypeStruct(RIMS, F32),
            pltpu.VMEM((2, 2, 2 * NQ * ROWS, HALF * ROWS), BF16),
            pltpu.VMEM((2, 2, 2 * NQ * 8, HALF * 8), BF16),
            pltpu.VMEM((2, 2, 3 * COLS, COLS), BF16),
            pltpu.VMEM((256, 128), BF16),
            pltpu.VMEM((5, 2, 2, ROWS, 128), F32),
            pltpu.VMEM((2, HALF + 1, 2, ROWS, 128), F32),
            pltpu.VMEM(HALVES, BF16),
            pltpu.VMEM(HALVES, BF16),
        ),
        in_specs=[VMEM] * 3,
        out_specs=[VMEM] * 10,
        compiler_params=params_of(8),
        name="prepare",
    )(x0, params, couple_weight)


def join(strips, west, east, low_rows, high_rows):
    return pl.pallas_call(
        join_kernel,
        out_shape=(
            jax.ShapeDtypeStruct((STRIPS, ROWS, 128), F32),
            jax.ShapeDtypeStruct(RIMS, F32),
            jax.ShapeDtypeStruct(RIMS, F32),
        ),
        in_specs=[VMEM] * 5,
        out_specs=[VMEM] * 3,
        input_output_aliases={3: 1, 4: 2},
        compiler_params=params_of(8),
        name="join",
    )(strips, west, east, low_rows, high_rows)


def inner(strips, x0, xhi, xlo, par, coef, weights, narrow, sides, strip_sides):
    flat = HALF * ROWS
    return pl.pallas_call(
        inner_kernel,
        out_shape=(pltpu.VMEM(FRAME, F32), pltpu.VMEM(HALVES, BF16), pltpu.VMEM(HALVES, BF16))
        + (pltpu.VMEM(FRAME, F32),) * 4
        + (pltpu.VMEM(STRIP, F32),) * 4
        + (pltpu.VMEM((2, NQ * ROWS, COLS), F32), pltpu.VMEM((2, NQ * 8 + 16, COLS), F32)),
        in_specs=[VMEM] * 10,
        out_specs=[VMEM] * 13,
        input_output_aliases={1: 0, 2: 1, 3: 2},
        scratch_shapes=[
            pltpu.VMEM((LEV, 2, ROWS, 128), F32),
            pltpu.VMEM((HALF, ROWS, 128), F32),
            pltpu.VMEM((6, ROWS, 128), F32),
            pltpu.VMEM((HALF + 1, ROWS, 128), F32),
            pltpu.VMEM((flat, 256), BF16),
            pltpu.VMEM((2, 2, flat, COLS), F32),
            pltpu.VMEM((flat, 128), F32),
        ],
        compiler_params=params_of(20),
        name="inner",
    )(strips, x0, xhi, xlo, par, coef, weights, narrow, sides, strip_sides)


def outer(*args):
    flat = HALF * 8
    return pl.pallas_call(
        outer_kernel,
        out_shape=(
            jax.ShapeDtypeStruct((1, 2, LEV, ROWS, COLS), F32),
            jax.ShapeDtypeStruct((NQ, ROWS, COLS), F32),
            jax.ShapeDtypeStruct((ROWS, 128), F32),
        ) + (pltpu.VMEM(FRAME, F32),) * 5 + (pltpu.VMEM(STRIP, F32),) * 4,
        in_specs=[VMEM] * 18,
        out_specs=[HBM, VMEM, VMEM] + [VMEM] * 9,
        input_output_aliases={9 + n: 3 + n for n in range(9)},
        scratch_shapes=[
            pltpu.VMEM((LEV, 2, 8, 128), F32),
            pltpu.VMEM((HALF, 8, 128), F32),
            pltpu.VMEM((6, 2, 2, 16, 128), F32),
            pltpu.VMEM((2, HALF + 1, 2, 16, 128), F32),
            pltpu.VMEM((6, 16, 128), F32),
            pltpu.VMEM((HALF + 1, 16, 128), F32),
            pltpu.VMEM((2, LEV, 2, 8, 128), F32),
            pltpu.VMEM((2, 2, flat, COLS), BF16),
            pltpu.VMEM((2, 2, flat, COLS), BF16),
            pltpu.VMEM((HALF, 8, 128), F32),
            pltpu.VMEM((flat, 256), BF16),
            pltpu.VMEM((2, 2, flat, COLS), F32),
            pltpu.VMEM((flat, 128), F32),
            pltpu.VMEM((STEPS, NQ, 2, TALL, 128), F32),
            pltpu.SemaphoreType.DMA((2, 2)),
        ],
        compiler_params=params_of(20),
        name="outer",
    )(*args)


def local(state, params, couple_weight, weight_table, intersection_map, sea_mask):
    lon, lat = lax.axis_size("lon"), lax.axis_size("lat")
    x0, strips = load(state, params)
    west = lax.ppermute(strips, "lon", ring(lon, 1, True))
    east = lax.ppermute(strips, "lon", ring(lon, -1, True))
    low_rows, high_rows, weights, narrow, sides, strip_sides, par, coef, xhi, xlo = prepare(
        x0, params, couple_weight
    )
    strips, low_rows, high_rows = join(strips, west, east, low_rows, high_rows)
    below = lax.ppermute(high_rows, "lat", ring(lat, 1, False))
    above = lax.ppermute(low_rows, "lat", ring(lat, -1, False))
    x0, _, _, *frames, sums, middle = inner(
        strips, x0, xhi, xlo, par, coef, weights, narrow, sides, strip_sides
    )
    new_state, mean, edges, *_ = outer(
        below, above, strips, params, sums, middle, narrow, sides, strip_sides, x0, *frames
    )
    received = lax.ppermute(mean, "comp", [(0, 1), (1, 0)])

    def across(step):
        return [(a * 2 + s, b * 2 + 1 - s) for a, b in ring(lon, step, True) for s in range(2)]

    west_edges = lax.ppermute(edges, ("lon", "comp"), across(1))
    east_edges = lax.ppermute(edges, ("lon", "comp"), across(-1))
    coupled = pl.pallas_call(
        remap_kernel,
        out_shape=jax.ShapeDtypeStruct((1, NQ, ROWS, COLS), F32),
        in_specs=[SMEM] + [VMEM] * 5,
        out_specs=VMEM,
        compiler_params=params_of(16),
        name="remap",
    )(weight_table, received, west_edges, east_edges, intersection_map, sea_mask)
    return new_state, coupled


def solution(mesh):
    placed = (
        P("comp", None, None, "lat", "lon"),
        P("comp", None, None, "lat", "lon"),
        P("comp", None, None, None),
        P("comp", None, None),
        P("comp", "lat", "lon"),
        P("comp", "lat", "lon"),
    )
    return jax.shard_map(
        local,
        mesh=mesh,
        in_specs=placed,
        out_specs=(P("comp", None, None, "lat", "lon"), P("comp", None, "lat", "lon")),
        check_vma=False,
    )
```

```python
import jax
import jax.numpy as jnp
from jax import lax
from jax.experimental import pallas as pl
from jax.experimental.pallas import tpu as pltpu
from jax.sharding import PartitionSpec as P

STEPS = 4
LEV = 64
HALF = LEV // 2
ROWS = 16
HALO = 4
COLS = 256
NQ = 8
OFF = 8
TALL = 32
PLANES = LEV + 3
STRIPS = HALF // 2 + 2
VMEM = pl.BlockSpec(memory_space=pltpu.VMEM)
SMEM = pl.BlockSpec(memory_space=pltpu.SMEM)
HBM = pl.BlockSpec(memory_space=pltpu.HBM)
BF16 = jnp.bfloat16
F32 = jnp.float32


def lanes():
    return lax.broadcasted_iota(jnp.int32, (8, 128), 1)


def subs():
    return lax.broadcasted_iota(jnp.int32, (8, 128), 0)


def level_of(level, h):
    return level if h == 0 else LEV - 1 - level


def halves(value):
    high = value.astype(BF16)
    return high, (value - high.astype(F32)).astype(BF16)


def params_of(vmem):
    return pltpu.CompilerParams(vmem_limit_bytes=vmem * 2**20)


def roll(value, shift):
    return pltpu.roll(value, shift % 128, 1)


def load_kernel(state, params, x0, strips, near, sem, near_sem):
    lane = lanes()
    part = LEV // 4
    copies = {}
    for n in (0, 3, 1, 2):
        for f in range(2):
            for c in range(2):
                copies[n, f, c] = pltpu.make_async_copy(
                    state.at[0, f, pl.ds(part * n, part), :, pl.ds(128 * c, 128)],
                    x0.at[f, pl.ds(part * n, part), c, pl.ds(OFF, ROWS)],
                    sem.at[n, f, c],
                )
                copies[n, f, c].start()
    small = pltpu.make_async_copy(params.at[0], near, near_sem)
    small.start()

    def place(total, source, index):
        ring = jnp.where(lane >= 124, source[1], source[0])
        first = roll(ring, 16 * index + 4)
        second = roll(ring, 16 * index + 12)
        inside = (lane >= 16 * index) & (lane < 16 * index + 16)
        pair = jnp.where((lane & 8) == 0, first, second)
        return pair if total is None else jnp.where(inside, pair, total)

    def strip(i, carry):
        made = []
        for block in (i * 2, i * 2 + 1):
            for rt in range(2):
                at = OFF + 8 * rt
                total = None
                for lq in range(2):
                    for f in range(2):
                        for h in range(2):
                            lam = level_of(block * 2 + lq, h)
                            source = [x0[f, lam, c, at:at + 8] for c in range(2)]
                            total = place(total, source, lq * 4 + f * 2 + h)
                made.append((block, rt, total))
        for block, rt, total in made:
            strips[block, 8 * rt:8 * rt + 8] = total
        return carry

    for n in range(2):
        for m in (n, 3 - n):
            for f in range(2):
                for c in range(2):
                    copies[m, f, c].wait()
        lax.fori_loop(n * part // 4, (n + 1) * part // 4, strip, 0)
    small.wait()
    for rt in range(2):
        rows = slice(8 * rt, 8 * rt + 8)
        total = None
        for lq in range(2):
            for f in range(2):
                for h in range(2):
                    source = [near[lq, f, rows, 128 * c:128 * c + 128] for c in range(2)]
                    total = place(total, source, lq * 4 + f * 2 + h)
        strips[HALF // 2, rows] = total
        total = jnp.zeros((8, 128), F32)
        for f in range(2):
            source = [near[2, f, rows, 128 * c:128 * c + 128] for c in range(2)]
            total = place(total, source, f * 2)
        strips[HALF // 2 + 1, rows] = total


def join_kernel(strips, west, east, low_in, high_in, joined, low_rows, high_rows):
    place = lanes() & 15
    for block in range(STRIPS):
        for rt in range(2):
            rows = slice(8 * rt, 8 * rt + 8)
            joined[block, rows] = jnp.where(
                place < 4, west[block, rows], jnp.where(place >= 12, east[block, rows], strips[block, rows])
            )
        cols = slice(128 * (block % 2), 128 * (block % 2) + 128)
        low_rows[2 * PLANES + block // 2, :, cols] = joined[block, 0:HALO]
        high_rows[2 * PLANES + block // 2, :, cols] = joined[block, ROWS - HALO:ROWS]


def kron_weights(couple_weight, out, rows):
    width = HALF * rows
    level = lax.broadcasted_iota(jnp.int32, (LEV, width), 0)
    place = lax.broadcasted_iota(jnp.int32, (LEV, width), 1)
    spread = []
    for h in range(2):
        first = rows * level_of(level, h)
        spread.append(((place >= first) & (place < first + rows)).astype(F32).astype(BF16))
    row = lax.broadcasted_iota(jnp.int32, (rows, width), 0)
    within = lax.broadcasted_iota(jnp.int32, (rows, width), 1) & (rows - 1)
    keep = within == row
    for f in range(2):
        for n, part in enumerate(halves(couple_weight[0, :, f, :])):
            for h in range(2):
                wide = jnp.dot(part, spread[h], preferred_element_type=F32)
                for q in range(0, NQ, 2):
                    at = n * NQ * rows + q * rows
                    pair = [jnp.where(keep, wide[q + i:q + i + 1], 0.0) for i in range(2)]
                    out[f, h, at:at + 2 * rows] = jnp.concatenate(pair, axis=0).astype(BF16)


def prepare_kernel(x0, params, couple_weight,
                   low_rows, high_rows, weights, narrow, sides, strip_sides, par, coef, xhi, xlo):
    def some(level, carry):
        at = pl.ds(pl.multiple_of(level * ROWS, 16), ROWS)
        for f in range(2):
            for h in range(2):
                lam = level_of(level, h)
                for c in range(2):
                    cols = slice(128 * c, 128 * c + 128)
                    value = x0[f, lam, c, OFF:OFF + ROWS]
                    high, low = halves(value)
                    xhi[f, h, at, cols] = high
                    xlo[f, h, at, cols] = low
                    low_rows[f * PLANES + lam, :, cols] = x0[f, lam, c, OFF:OFF + HALO]
                    high_rows[f * PLANES + lam, :, cols] = x0[f, lam, c, OFF + ROWS - HALO:OFF + ROWS]
        return carry

    for f in range(2):
        for kind in range(3):
            low_rows[f * PLANES + LEV + kind] = params[0, kind, f, 0:HALO]
            high_rows[f * PLANES + LEV + kind] = params[0, kind, f, ROWS - HALO:ROWS]
    columns = [(f, c, rt) for f in range(2) for c in range(2) for rt in range(2)]
    for f, c, rt in columns:
        rows = slice(8 * rt, 8 * rt + 8)
        h, k, g = [params[0, kind, f, rows, 128 * c:128 * c + 128] for kind in range(3)]
        for n, value in enumerate((h, k, g, 1.0 / k, 1.0 - 4.0 * h)):
            par[n, f, c, rows] = value

    def pivots(i, carry):
        out = []
        for n, (f, c, rt) in enumerate(columns):
            rows = slice(8 * rt, 8 * rt + 8)
            out.append(pivot_levels(coef, (f,), (c, rows), q[n], carry[n], i * 2, 2))
        for u in range(2):
            some(i * 2 + u, 0)
        return tuple(out)

    q = [ratio(par[1, f, c, 8 * rt:8 * rt + 8]) for f, c, rt in columns]
    lax.fori_loop(0, HALF // 2, pivots, tuple(q))
    for f, c, rt in columns:
        rows = slice(8 * rt, 8 * rt + 8)
        m = coef[f, HALF - 1, c, rows]
        coef[f, HALF, c, rows] = m / (1.0 - m * m)
    kron_weights(couple_weight, weights, ROWS)
    kron_weights(couple_weight, narrow, 8)
    row = lax.broadcasted_iota(jnp.int32, (COLS, COLS), 0)
    col = lax.broadcasted_iota(jnp.int32, (COLS, COLS), 1)
    inner = (jnp.abs(row - col) == 1).astype(F32).astype(jnp.bfloat16)
    lane = row & 127
    for f in range(2):
        for h in range(2):
            base = f * 32 + h * 16
            rim = ((lane == base + 3) & (col == 0)) | ((lane == base + 12) & (col == COLS - 1))
            sides[f, h, 0:COLS] = inner
            sides[f, h, COLS:2 * COLS] = inner
            sides[f, h, 2 * COLS:3 * COLS] = rim.astype(F32).astype(jnp.bfloat16)
    near = jnp.abs((row & 127) - col)[:, 0:128] == 1
    strip_sides[...] = near.astype(F32).astype(jnp.bfloat16)

def ratio(k):
    root = jnp.sqrt(1.0 + 4.0 * k) + 1.0
    return 4.0 * k / (root * root)


def pivot_levels(ref, index, rows, q, power, first, count):
    square = q * q
    for u in range(count):
        above = power * square
        ref[*index, first + u, *rows] = q * (1.0 + power) / (1.0 + above)
        power = above
    return power


def strip_params(spar):
    for rt in range(2):
        rows = slice(8 * rt, 8 * rt + 8)
        k = spar[1, rows]
        k = jnp.where(k > 0.0, k, 1.0)
        spar[5, rows] = ratio(k)
        spar[3, rows] = 1.0 / k
        spar[4, rows] = 1.0 - 4.0 * spar[0, rows]


def strip_pivots(spar, scoef, first, count, carry):
    out = []
    for rt in range(2):
        rows = slice(8 * rt, 8 * rt + 8)
        out.append(pivot_levels(scoef, (), (rows,), spar[5, rows], carry[rt], first, count))
    return tuple(out)


def strip_closing(scoef):
    for rt in range(2):
        rows = slice(8 * rt, 8 * rt + 8)
        m = scoef[HALF - 1, rows]
        scoef[HALF, rows] = m / (1.0 - m * m)


def swap_ends(value):
    return jnp.where((lanes() & 16) == 0, roll(value, -16), roll(value, 16))


def inner_kernel(strips, x0_in, xhi_in, xlo_in, par, coef, weights, narrow, sides, strip_sides,
                 x0, xhi, xlo, x1, x2, x3, x4, t0, t1, t2, t3, sums, middle,
                 xe, te, spar, scoef, tsplit, beside, strip_beside):
    xs, ts = (x0, x1, x2, x3, x4), (t0, t1, t2, t3)
    sub = subs()
    zero = jnp.zeros((8, 128), F32)

    for rt in range(2):
        rows = slice(8 * rt, 8 * rt + 8)
        spar[0, rows] = strips[HALF // 2, rows]
        spar[1, rows] = roll(strips[HALF // 2, rows], 64)
        spar[2, rows] = strips[HALF // 2 + 1, rows]
    strip_params(spar)

    def unstrip(i, carry):
        levels = []
        for u in range(4):
            block = i * 4 + u
            for lq in range(2):
                tiles = [roll(strips[block, 8 * rt:8 * rt + 8], 64 * lq) for rt in range(2)]
                levels.append((block * 2 + lq, tiles))
        for level, tiles in levels:
            for rt in range(2):
                t0[level, OFF + 8 * rt:OFF + 8 * rt + 8] = tiles[rt]
            split_strip(level, tiles)
        return strip_pivots(spar, scoef, i * 8, 8, carry)

    def split_strip(level, tiles):
        at = pl.ds(pl.multiple_of(level * ROWS, 16), ROWS)
        high, low = halves(jnp.concatenate(tiles, axis=0))
        tsplit[at, 0:128] = high
        tsplit[at, 128:256] = low

    lax.fori_loop(0, HALF // 8, unstrip, (spar[5, 0:8], spar[5, 8:16]))
    strip_closing(scoef)

    def vertical(load, rt):
        at = OFF + 8 * rt
        up, down = load(at - 1), load(at + 1)
        if rt == 0:
            up = jnp.where(sub == 0, 0.0, up)
        else:
            down = jnp.where(sub == 7, 0.0, down)
        return up + down

    def neighbours():
        def part(i, carry):
            at = pl.ds(pl.multiple_of(i * 256, 16), 256)
            for f in range(2):
                for h in range(2):
                    value = jnp.concatenate([xhi[f, h, at], xlo[f, h, at], tsplit[at]], axis=1)
                    beside[f, h, at] = jnp.dot(value, sides[f, h], preferred_element_type=F32)
            strip_beside[at] = jnp.dot(tsplit[at], strip_sides[...], preferred_element_type=F32)
            return carry

        lax.fori_loop(0, HALF * ROWS // 256, part, 0)

    def packages(n):
        total = None
        for f in range(2):
            for h in range(2):
                both = jnp.dot(weights[f, h], xhi[f, h], preferred_element_type=F32)
                high = jnp.dot(weights[f, h, :NQ * ROWS], xlo[f, h], preferred_element_type=F32)
                value = (both[NQ * ROWS:] + high) + both[:NQ * ROWS]
                total = value if total is None else total + value
        sums[n] = total

    def main_field(x, xn, f, halve):
        tiles = [(c, rt, slice(8 * rt, 8 * rt + 8), OFF + 8 * rt) for c in range(2) for rt in range(2)]
        diff = [par[0, f, c, rows] for c, rt, rows, at in tiles]
        keep = [par[4, f, c, rows] for c, rt, rows, at in tiles]

        def forward(i, carry):
            carry = list(carry)
            for u in range(4):
                level = i * 4 + u
                for n, (c, rt, rows, at) in enumerate(tiles):
                    m = coef[f, level, c, rows]
                    flat = pl.ds(pl.multiple_of(level * ROWS, 8) + 8 * rt, 8)
                    for h in range(2):
                        lam = level_of(level, h)
                        around = vertical(lambda r: x[f, lam, c, r:r + 8], rt)
                        around = around + beside[f, h, flat, 128 * c:128 * c + 128]
                        e = (keep[n] * x[f, lam, c, at:at + 8] + diff[n] * around) + carry[h * 4 + n]
                        xe[lam, c, rows] = e
                        carry[h * 4 + n] = m * e
            return tuple(carry)

        start = tuple(par[2, f, c, rows] for c, rt, rows, at in tiles) + (zero,) * 4
        ends = lax.fori_loop(0, HALF // 4, forward, start)
        inv = [par[3, f, c, rows] for c, rt, rows, at in tiles]

        def finish(level, h, z):
            lam = level_of(level, h)
            flat = pl.ds(pl.multiple_of(level * ROWS, 16), ROWS)
            for c in range(2):
                y = []
                for rt in range(2):
                    v = z[h * 4 + 2 * c + rt] * inv[2 * c + rt]
                    xn[f, lam, c, OFF + 8 * rt:OFF + 8 * rt + 8] = v
                    y.append(v)
                if not halve:
                    continue
                high, low = halves(jnp.concatenate(y, axis=0))
                xhi[f, h, flat, 128 * c:128 * c + 128] = high
                xlo[f, h, flat, 128 * c:128 * c + 128] = low

        z = [None] * 8
        for h in range(2):
            for n, (c, rt, rows, at) in enumerate(tiles):
                z[h * 4 + n] = coef[f, HALF, c, rows] * (xe[HALF - 1 + h, c, rows] + ends[(1 - h) * 4 + n])
        for h in range(2):
            finish(HALF - 1, h, z)

        def back_level(level, z):
            out = [None] * 8
            for h in range(2):
                lam = level_of(level, h)
                for n, (c, rt, rows, at) in enumerate(tiles):
                    out[h * 4 + n] = coef[f, level, c, rows] * (xe[lam, c, rows] + z[h * 4 + n])
                finish(level, h, out)
            return tuple(out)

        def back(i, z):
            for u in range(3):
                z = back_level(HALF - 2 - (i * 3 + u), z)
            return z

        z = lax.fori_loop(0, HALF // 3, back, tuple(z))
        back_level(0, z)

    def strip_step(t, tn):
        tiles = [slice(8 * rt, 8 * rt + 8) for rt in range(2)]
        diff = [spar[0, rows] for rows in tiles]
        inv = [spar[3, rows] for rows in tiles]
        keep = [spar[4, rows] for rows in tiles]

        def forward(i, carry):
            carry = list(carry)
            for u in range(8):
                level = i * 8 + u
                for rt, rows in enumerate(tiles):
                    flat = pl.ds(pl.multiple_of(level * ROWS, 8) + 8 * rt, 8)
                    around = vertical(lambda r: t[level, r:r + 8], rt) + strip_beside[flat]
                    e = (keep[rt] * t[level, OFF + 8 * rt:OFF + 8 * rt + 8] + diff[rt] * around) + carry[rt]
                    te[level, rows] = e
                    carry[rt] = scoef[level, rows] * e
            return tuple(carry)

        ends = lax.fori_loop(0, HALF // 8, forward, tuple(spar[2, rows] for rows in tiles))
        def finish(level, z):
            y = [z[rt] * inv[rt] for rt in range(2)]
            for rt in range(2):
                tn[level, OFF + 8 * rt:OFF + 8 * rt + 8] = y[rt]
            split_strip(level, y)

        z = [scoef[HALF, rows] * (te[HALF - 1, rows] + swap_ends(ends[rt])) for rt, rows in enumerate(tiles)]
        finish(HALF - 1, z)

        def back_level(level, z):
            out = [scoef[level, rows] * (te[level, rows] + z[rt]) for rt, rows in enumerate(tiles)]
            finish(level, out)
            return tuple(out)

        def back(i, z):
            for u in range(10):
                z = back_level(HALF - 2 - (i * 10 + u), z)
            return z

        z = lax.fori_loop(0, HALF // 10, back, tuple(z))
        back_level(0, z)

    begin, rows8 = OFF + 4, slice(4, 12)

    def halve_middle(x, t):
        def some(i, carry):
            at = pl.ds(pl.multiple_of(i * 16, 16), 16)
            for f in range(2):
                for h in range(2):
                    for c in range(2):
                        pair = [x[f, level_of(i * 2 + u, h), c, begin:begin + 8] for u in range(2)]
                        high, low = halves(jnp.concatenate(pair, axis=0))
                        xhi[f, h, at, 128 * c:128 * c + 128] = high
                        xlo[f, h, at, 128 * c:128 * c + 128] = low
            if t is not None:
                pair = [t[i * 2 + u, begin:begin + 8] for u in range(2)]
                high, low = halves(jnp.concatenate(pair, axis=0))
                tsplit[at, 0:128] = high
                tsplit[at, 128:256] = low
            return carry

        lax.fori_loop(0, HALF // 2, some, 0)

    def neighbours_middle():
        for f in range(2):
            for h in range(2):
                value = jnp.concatenate([xhi[f, h, 0:256], xlo[f, h, 0:256], tsplit[0:256]], axis=1)
                beside[f, h, 0:256] = jnp.dot(value, sides[f, h], preferred_element_type=F32)

    def packages_middle(n):
        total = None
        for f in range(2):
            for h in range(2):
                both = jnp.dot(narrow[f, h], xhi[f, h, 0:256], preferred_element_type=F32)
                high = jnp.dot(narrow[f, h, :NQ * 8], xlo[f, h, 0:256], preferred_element_type=F32)
                value = (both[NQ * 8:] + high) + both[:NQ * 8]
                total = value if total is None else total + value
        middle[n, 8:8 + NQ * 8] = total

    def main_middle(x, xn, f):
        diff = [par[0, f, c, rows8] for c in range(2)]
        keep = [par[4, f, c, rows8] for c in range(2)]
        inv = [par[3, f, c, rows8] for c in range(2)]

        def forward(i, carry):
            carry = list(carry)
            for u in range(8):
                level = i * 8 + u
                flat = pl.ds(pl.multiple_of(level * 8, 8), 8)
                for c in range(2):
                    m = coef[f, level, c, rows8]
                    for h in range(2):
                        lam = level_of(level, h)
                        around = x[f, lam, c, begin - 1:begin + 7] + x[f, lam, c, begin + 1:begin + 9]
                        around = around + beside[f, h, flat, 128 * c:128 * c + 128]
                        e = (keep[c] * x[f, lam, c, begin:begin + 8] + diff[c] * around) + carry[h * 2 + c]
                        xe[lam, c, 0:8] = e
                        carry[h * 2 + c] = m * e
            return tuple(carry)

        start = (par[2, f, 0, rows8], par[2, f, 1, rows8], zero, zero)
        ends = lax.fori_loop(0, HALF // 8, forward, start)
        z = []
        for h in range(2):
            for c in range(2):
                v = coef[f, HALF, c, rows8] * (xe[HALF - 1 + h, c, 0:8] + ends[(1 - h) * 2 + c])
                xn[f, HALF - 1 + h, c, begin:begin + 8] = v * inv[c]
                z.append(v)

        def back_level(level, z):
            out = [None] * 4
            for c in range(2):
                m = coef[f, level, c, rows8]
                for h in range(2):
                    lam = level_of(level, h)
                    v = m * (xe[lam, c, 0:8] + z[h * 2 + c])
                    xn[f, lam, c, begin:begin + 8] = v * inv[c]
                    out[h * 2 + c] = v
            return tuple(out)

        def back(i, z):
            for u in range(10):
                z = back_level(HALF - 2 - (i * 10 + u), z)
            return z

        z = lax.fori_loop(0, HALF // 10, back, tuple(z))
        back_level(0, z)

    for step in range(STEPS - 1):
        neighbours()
        if step > 0:
            packages(step - 1)
        for f in range(2):
            main_field(xs[step], xs[step + 1], f, step < STEPS - 2)
        strip_step(ts[step], ts[step + 1])
    halve_middle(x3, t3)
    neighbours_middle()
    packages_middle(0)
    for f in range(2):
        main_middle(x3, x4, f)
    halve_middle(x4, None)
    packages_middle(1)


def outer_kernel(below, above, strips, params, sums, middle, narrow, sides, strip_sides,
                 i0, i1, i2, i3, i4, j0, j1, j2, j3,
                 new_state, mean, edges, x0, x1, x2, x3, x4, t0, t1, t2, t3,
                 xe, te, par, coef, spar, scoef, centre, xhi, xlo, tcentre, tsplit, beside, strip_beside, patch, sem):
    xs, ts = (x0, x1, x2, x3, x4), (t0, t1, t2, t3)
    lane, sub = lanes(), subs()
    top = sub < 4
    zero = jnp.zeros((8, 128), F32)
    here = lax.axis_index("lat")
    outside = [jnp.full((HALO, 128), here, jnp.int32) == end for end in (0, lax.axis_size("lat") - 1)]

    def rim(n, plane, c):
        ref = (below, above)[n]
        return jnp.where(outside[n], 0.0, ref[plane, :, 128 * c:128 * c + 128])

    def strip_rim(n, block):
        return rim(n, 2 * PLANES + block // 2, block % 2)

    for n, (block, shift) in enumerate(((HALF // 2, 0), (HALF // 2, 64), (HALF // 2 + 1, 0))):
        spar[n, 0:4] = pltpu.roll(strip_rim(0, block), shift, 1)
        spar[n, 4:8] = pltpu.roll(strips[block, 0:4], shift, 1)
        spar[n, 8:12] = pltpu.roll(strips[block, 12:16], shift, 1)
        spar[n, 12:16] = pltpu.roll(strip_rim(1, block), shift, 1)
    strip_params(spar)
    columns = [(f, c, rt) for f in range(2) for c in range(2) for rt in range(2)]
    for f in range(2):
        for c in range(2):
            cols = slice(128 * c, 128 * c + 128)
            for n in range(3):
                par[n, f, c, 0:4] = rim(0, f * PLANES + LEV + n, c)
                par[n, f, c, 4:8] = params[0, n, f, 0:4, cols]
                par[n, f, c, 8:12] = params[0, n, f, 12:16, cols]
                par[n, f, c, 12:16] = rim(1, f * PLANES + LEV + n, c)
    for f, c, rt in columns:
        rows = slice(8 * rt, 8 * rt + 8)
        k = par[1, f, c, rows]
        k = jnp.where(k > 0.0, k, 1.0)
        par[5, f, c, rows] = ratio(k)
        par[3, f, c, rows] = 1.0 / k
        par[4, f, c, rows] = 1.0 - 4.0 * par[0, f, c, rows]

    def pivots(i, carry):
        out = []
        for n, (f, c, rt) in enumerate(columns):
            rows = slice(8 * rt, 8 * rt + 8)
            out.append(pivot_levels(coef, (f,), (c, rows), par[5, f, c, rows], carry[n], i * 4, 4))
        out.extend(strip_pivots(spar, scoef, i * 4, 4, carry[len(columns):]))
        for u in range(4):
            for f in range(2):
                for h in range(2):
                    lam = level_of(i * 4 + u, h)
                    for c in range(2):
                        x0[f, lam, c, OFF - HALO:OFF] = rim(0, f * PLANES + lam, c)
                        x0[f, lam, c, OFF + ROWS:OFF + ROWS + HALO] = rim(1, f * PLANES + lam, c)
        rims = []
        for c in range(2):
            for lq in range(2):
                for n in range(2):
                    rims.append(pltpu.roll(rim(n, 2 * PLANES + i, c), 64 * lq, 1))
        for n in range(4):
            t0[i * 4 + n, OFF - HALO:OFF] = rims[2 * n]
            t0[i * 4 + n, OFF + ROWS:OFF + ROWS + HALO] = rims[2 * n + 1]
        return tuple(out)

    start = [par[5, f, c, 8 * rt:8 * rt + 8] for f, c, rt in columns] + [spar[5, 0:8], spar[5, 8:16]]
    lax.fori_loop(0, HALF // 4, pivots, tuple(start))
    for f, c, rt in columns:
        rows = slice(8 * rt, 8 * rt + 8)
        m = coef[f, HALF - 1, c, rows]
        coef[f, HALF, c, rows] = m / (1.0 - m * m)
    strip_closing(scoef)

    def gather(x, step):
        a, b = OFF - 4 + step, OFF + 12 - step

        def some(i, carry):
            at = pl.ds(pl.multiple_of(i * 16, 16), 16)
            for f in range(2):
                for h in range(2):
                    for c in range(2):
                        pair = []
                        for u in range(2):
                            lam = level_of(i * 2 + u, h)
                            v = jnp.where(top, x[f, lam, c, a:a + 8], x[f, lam, c, b:b + 8])
                            centre[f, lam, c] = v
                            pair.append(v)
                        high, low = halves(jnp.concatenate(pair, axis=0))
                        xhi[f, h, at, 128 * c:128 * c + 128] = high
                        xlo[f, h, at, 128 * c:128 * c + 128] = low
            return carry

        lax.fori_loop(0, HALF // 2, some, 0)

    def gather_strip(t, step):
        a, b = OFF - 4 + step, OFF + 12 - step

        def some(i, carry):
            at = pl.ds(pl.multiple_of(i * 16, 16), 16)
            pair = []
            for u in range(2):
                v = jnp.where(top, t[i * 2 + u, a:a + 8], t[i * 2 + u, b:b + 8])
                tcentre[i * 2 + u] = v
                pair.append(v)
            high, low = halves(jnp.concatenate(pair, axis=0))
            tsplit[at, 0:128] = high
            tsplit[at, 128:256] = low
            return carry

        lax.fori_loop(0, HALF // 2, some, 0)

    def neighbours():
        for f in range(2):
            for h in range(2):
                value = jnp.concatenate([xhi[f, h], xlo[f, h], tsplit[...]], axis=1)
                beside[f, h] = jnp.dot(value, sides[f, h], preferred_element_type=F32)
        strip_beside[...] = jnp.dot(tsplit[...], strip_sides[...], preferred_element_type=F32)

    def packages(n, step):
        a, b = OFF - 4 + step, OFF + 12 - step
        total = None
        for f in range(2):
            for h in range(2):
                both = jnp.dot(narrow[f, h], xhi[f, h], preferred_element_type=F32)
                high = jnp.dot(narrow[f, h, :NQ * 8], xlo[f, h], preferred_element_type=F32)
                value = (both[NQ * 8:] + high) + both[:NQ * 8]
                total = value if total is None else total + value
        for q in range(NQ):
            for c in range(2):
                v = total[q * 8:q * 8 + 8, 128 * c:128 * c + 128]
                pltpu.store(patch.at[n, q, c, pl.ds(a, 8)], v, mask=top)
                pltpu.store(patch.at[n, q, c, pl.ds(b, 8)], v, mask=sub >= 4)

    def main_field(x, xn, f, step):
        a, b = OFF - 4 + step, OFF + 12 - step

        def mine(load):
            return jnp.where(top, load(slice(step, step + 8)), load(slice(8 - step, 16 - step)))

        def put(lam, c, v):
            pltpu.store(xn.at[f, lam, c, pl.ds(a, 8)], v, mask=top)
            pltpu.store(xn.at[f, lam, c, pl.ds(b, 8)], v, mask=sub >= 4)

        diff = [mine(lambda r: par[0, f, c, r]) for c in range(2)]
        keep = [mine(lambda r: par[4, f, c, r]) for c in range(2)]
        inv = [mine(lambda r: par[3, f, c, r]) for c in range(2)]

        def forward(i, carry):
            carry = list(carry)
            for u in range(4):
                level = i * 4 + u
                m = [mine(lambda r: coef[f, level, c, r]) for c in range(2)]
                flat = pl.ds(pl.multiple_of(level * 8, 8), 8)
                for h in range(2):
                    lam = level_of(level, h)
                    for c in range(2):
                        around = jnp.where(
                            top,
                            x[f, lam, c, a - 1:a + 7] + x[f, lam, c, a + 1:a + 9],
                            x[f, lam, c, b - 1:b + 7] + x[f, lam, c, b + 1:b + 9],
                        ) + beside[f, h, flat, 128 * c:128 * c + 128]
                        e = (keep[c] * centre[f, lam, c] + diff[c] * around) + carry[h * 2 + c]
                        xe[lam, c] = e
                        carry[h * 2 + c] = m[c] * e
            return tuple(carry)

        start = (mine(lambda r: par[2, f, 0, r]), mine(lambda r: par[2, f, 1, r]), zero, zero)
        ends = lax.fori_loop(0, HALF // 4, forward, start)
        z = []
        for h in range(2):
            for c in range(2):
                v = mine(lambda r: coef[f, HALF, c, r]) * (xe[HALF - 1 + h, c] + ends[(1 - h) * 2 + c])
                put(HALF - 1 + h, c, v * inv[c])
                z.append(v)

        def back_level(level, z):
            out = []
            m = [mine(lambda r: coef[f, level, c, r]) for c in range(2)]
            for h in range(2):
                lam = level_of(level, h)
                for c in range(2):
                    v = m[c] * (xe[lam, c] + z[h * 2 + c])
                    put(lam, c, v * inv[c])
                    out.append(v)
            return tuple(out)

        def back(i, z):
            for u in range(10):
                z = back_level(HALF - 2 - (i * 10 + u), z)
            return z

        z = lax.fori_loop(0, HALF // 10, back, tuple(z))
        back_level(0, z)

    def strip_step(t, tn, step):
        a, b = OFF - 4 + step, OFF + 12 - step

        def mine(load):
            return jnp.where(top, load(slice(step, step + 8)), load(slice(8 - step, 16 - step)))

        def put(level, v):
            pltpu.store(tn.at[level, pl.ds(a, 8)], v, mask=top)
            pltpu.store(tn.at[level, pl.ds(b, 8)], v, mask=sub >= 4)

        diff, keep, inv = [mine(lambda r: spar[n, r]) for n in (0, 4, 3)]

        def forward(i, carry):
            for u in range(16):
                level = i * 16 + u
                flat = pl.ds(pl.multiple_of(level * 8, 8), 8)
                around = jnp.where(
                    top,
                    t[level, a - 1:a + 7] + t[level, a + 1:a + 9],
                    t[level, b - 1:b + 7] + t[level, b + 1:b + 9],
                ) + strip_beside[flat]
                e = (keep * tcentre[level] + diff * around) + carry
                te[level] = e
                carry = mine(lambda r: scoef[level, r]) * e
            return carry

        end = lax.fori_loop(0, HALF // 16, forward, mine(lambda r: spar[2, r]))
        z = mine(lambda r: scoef[HALF, r]) * (te[HALF - 1] + swap_ends(end))
        put(HALF - 1, z * inv)

        def back_level(level, z):
            z = mine(lambda r: scoef[level, r]) * (te[level] + z)
            put(level, z * inv)
            return z

        def back(i, z):
            for u in range(10):
                z = back_level(HALF - 2 - (i * 10 + u), z)
            return z

        back_level(0, lax.fori_loop(0, HALF // 10, back, z))

    copies = []
    for step in range(1, STEPS + 1):
        gather(xs[step - 1], step)
        gather_strip(ts[step - 1], step)
        neighbours()
        if step > 1:
            packages(step - 2, step)
        for f in range(2):
            main_field(xs[step - 1], xs[step], f, step)
            if step < STEPS:
                continue
            for c in range(2):
                copies.append(pltpu.make_async_copy(
                    x4.at[f, :, c, pl.ds(OFF, ROWS)], new_state.at[0, f, :, :, pl.ds(128 * c, 128)], sem.at[f, c]
                ))
                copies[-1].start()
        if step < STEPS:
            strip_step(ts[step - 1], ts[step], step)
    gather(xs[STEPS], STEPS)
    packages(STEPS - 1, STEPS)
    for rt in range(2):
        total = zero
        for q in range(NQ):
            value = []
            for c in range(2):
                got = None
                for n in range(STEPS):
                    cols = slice(128 * c, 128 * c + 128)
                    if n < 2:
                        stale = sub < n + 1 if rt == 0 else sub >= 7 - n
                        own = sums[n, q * ROWS + 8 * rt:q * ROWS + 8 * rt + 8, cols]
                    else:
                        stale = top if rt == 0 else sub >= 4
                        own = middle[n - 2, 4 + 8 * q + 8 * rt:12 + 8 * q + 8 * rt, cols]
                    v = jnp.tanh(jnp.where(stale, patch[n, q, c, OFF + 8 * rt:OFF + 8 * rt + 8], own))
                    got = v if got is None else got + v
                value.append(got * (1.0 / STEPS))
                mean[q, 8 * rt:8 * rt + 8, 128 * c:128 * c + 128] = value[c]
            ring = jnp.where(lane >= 126, value[1], value[0])
            total = jnp.where((lane >= 4 * q) & (lane < 4 * q + 4), roll(ring, 4 * q + 2), total)
        edges[8 * rt:8 * rt + 8] = total
    for copy in copies:
        copy.wait()


def remap_kernel(table, received, west_edges, east_edges, codes, mask, out):
    lane = lanes()
    for rt in range(2):
        rows = slice(8 * rt, 8 * rt + 8)
        west_edge = west_edges[rows]
        east_edge = east_edges[rows]
        picks, first, second, sea = [], [], [], []
        for c in range(2):
            cols = slice(128 * c, 128 * c + 128)
            code = codes[0, rows, cols]
            offset = code & 3
            row = code >> 2
            w = []
            for j in range(2):
                v = jnp.full((8, 128), table[0, 0, j], F32)
                for n in range(1, 4):
                    v = jnp.where(row == n, table[0, n, j], v)
                w.append(v)
            first.append(w[0])
            second.append(w[1])
            picks.append([offset == n for n in range(1, 4)])
            sea.append(mask[0, rows, cols] == 1)
        for q in range(NQ):
            v = [received[q, rows, 128 * c:128 * c + 128] for c in range(2)]
            shifted = [[None] * 5, [None] * 5]
            for c in range(2):
                shifted[c][2] = v[c]
            for d in (1, 2):
                turned = [roll(u, d) for u in v]
                far = roll(west_edge, d - (4 * q + 2))
                shifted[0][2 - d] = jnp.where(lane < d, far, turned[0])
                shifted[1][2 - d] = jnp.where(lane < d, turned[0], turned[1])
                turned = [roll(u, -d) for u in v]
                far = roll(east_edge, 128 - d - (4 * q + 2))
                shifted[0][2 + d] = jnp.where(lane >= 128 - d, turned[1], turned[0])
                shifted[1][2 + d] = jnp.where(lane >= 128 - d, far, turned[1])
            for c in range(2):
                near, beyond = shifted[c][0], shifted[c][1]
                for n in range(1, 4):
                    near = jnp.where(picks[c][n - 1], shifted[c][n], near)
                    beyond = jnp.where(picks[c][n - 1], shifted[c][n + 1], beyond)
                value = first[c] * near + second[c] * beyond
                out[0, q, rows, 128 * c:128 * c + 128] = jnp.where(sea[c], value, 0.0)


def ring(count, step, periodic):
    pairs = [(i, i + step) for i in range(count)]
    if periodic:
        return [(a, b % count) for a, b in pairs]
    return [(a, b) for a, b in pairs if 0 <= b < count]


FRAME = (2, LEV, 2, TALL, 128)
STRIP = (HALF, TALL, 128)


RIMS = (2 * PLANES + STRIPS // 2, HALO, COLS)
HALVES = (2, 2, HALF * ROWS, COLS)


def load(state, params):
    return pl.pallas_call(
        load_kernel,
        out_shape=(pltpu.VMEM(FRAME, F32), jax.ShapeDtypeStruct((STRIPS, ROWS, 128), F32)),
        in_specs=[HBM, HBM],
        out_specs=[VMEM] * 2,
        scratch_shapes=[
            pltpu.VMEM((3, 2, ROWS, COLS), F32),
            pltpu.SemaphoreType.DMA((4, 2, 2)),
            pltpu.SemaphoreType.DMA,
        ],
        compiler_params=params_of(8),
        name="load",
    )(*[pltpu.with_memory_space_constraint(v, pltpu.HBM) for v in (state, params)])


def prepare(x0, params, couple_weight):
    return pl.pallas_call(
        prepare_kernel,
        out_shape=(
            jax.ShapeDtypeStruct(RIMS, F32),
            jax.ShapeDtypeStruct(RIMS, F32),
            pltpu.VMEM((2, 2, 2 * NQ * ROWS, HALF * ROWS), BF16),
            pltpu.VMEM((2, 2, 2 * NQ * 8, HALF * 8), BF16),
            pltpu.VMEM((2, 2, 3 * COLS, COLS), BF16),
            pltpu.VMEM((256, 128), BF16),
            pltpu.VMEM((5, 2, 2, ROWS, 128), F32),
            pltpu.VMEM((2, HALF + 1, 2, ROWS, 128), F32),
            pltpu.VMEM(HALVES, BF16),
            pltpu.VMEM(HALVES, BF16),
        ),
        in_specs=[VMEM] * 3,
        out_specs=[VMEM] * 10,
        compiler_params=params_of(8),
        name="prepare",
    )(x0, params, couple_weight)


def join(strips, west, east, low_rows, high_rows):
    return pl.pallas_call(
        join_kernel,
        out_shape=(
            jax.ShapeDtypeStruct((STRIPS, ROWS, 128), F32),
            jax.ShapeDtypeStruct(RIMS, F32),
            jax.ShapeDtypeStruct(RIMS, F32),
        ),
        in_specs=[VMEM] * 5,
        out_specs=[VMEM] * 3,
        input_output_aliases={3: 1, 4: 2},
        compiler_params=params_of(8),
        name="join",
    )(strips, west, east, low_rows, high_rows)


def inner(strips, x0, xhi, xlo, par, coef, weights, narrow, sides, strip_sides):
    flat = HALF * ROWS
    return pl.pallas_call(
        inner_kernel,
        out_shape=(pltpu.VMEM(FRAME, F32), pltpu.VMEM(HALVES, BF16), pltpu.VMEM(HALVES, BF16))
        + (pltpu.VMEM(FRAME, F32),) * 4
        + (pltpu.VMEM(STRIP, F32),) * 4
        + (pltpu.VMEM((2, NQ * ROWS, COLS), F32), pltpu.VMEM((2, NQ * 8 + 16, COLS), F32)),
        in_specs=[VMEM] * 10,
        out_specs=[VMEM] * 13,
        input_output_aliases={1: 0, 2: 1, 3: 2},
        scratch_shapes=[
            pltpu.VMEM((LEV, 2, ROWS, 128), F32),
            pltpu.VMEM((HALF, ROWS, 128), F32),
            pltpu.VMEM((6, ROWS, 128), F32),
            pltpu.VMEM((HALF + 1, ROWS, 128), F32),
            pltpu.VMEM((flat, 256), BF16),
            pltpu.VMEM((2, 2, flat, COLS), F32),
            pltpu.VMEM((flat, 128), F32),
        ],
        compiler_params=params_of(20),
        name="inner",
    )(strips, x0, xhi, xlo, par, coef, weights, narrow, sides, strip_sides)


def outer(*args):
    flat = HALF * 8
    return pl.pallas_call(
        outer_kernel,
        out_shape=(
            jax.ShapeDtypeStruct((1, 2, LEV, ROWS, COLS), F32),
            jax.ShapeDtypeStruct((NQ, ROWS, COLS), F32),
            jax.ShapeDtypeStruct((ROWS, 128), F32),
        ) + (pltpu.VMEM(FRAME, F32),) * 5 + (pltpu.VMEM(STRIP, F32),) * 4,
        in_specs=[VMEM] * 18,
        out_specs=[HBM, VMEM, VMEM] + [VMEM] * 9,
        input_output_aliases={9 + n: 3 + n for n in range(9)},
        scratch_shapes=[
            pltpu.VMEM((LEV, 2, 8, 128), F32),
            pltpu.VMEM((HALF, 8, 128), F32),
            pltpu.VMEM((6, 2, 2, 16, 128), F32),
            pltpu.VMEM((2, HALF + 1, 2, 16, 128), F32),
            pltpu.VMEM((6, 16, 128), F32),
            pltpu.VMEM((HALF + 1, 16, 128), F32),
            pltpu.VMEM((2, LEV, 2, 8, 128), F32),
            pltpu.VMEM((2, 2, flat, COLS), BF16),
            pltpu.VMEM((2, 2, flat, COLS), BF16),
            pltpu.VMEM((HALF, 8, 128), F32),
            pltpu.VMEM((flat, 256), BF16),
            pltpu.VMEM((2, 2, flat, COLS), F32),
            pltpu.VMEM((flat, 128), F32),
            pltpu.VMEM((STEPS, NQ, 2, TALL, 128), F32),
            pltpu.SemaphoreType.DMA((2, 2)),
        ],
        compiler_params=params_of(20),
        name="outer",
    )(*args)


def local(state, params, couple_weight, weight_table, intersection_map, sea_mask):
    lon, lat = lax.axis_size("lon"), lax.axis_size("lat")
    x0, strips = load(state, params)
    west = lax.ppermute(strips, "lon", ring(lon, 1, True))
    east = lax.ppermute(strips, "lon", ring(lon, -1, True))
    low_rows, high_rows, weights, narrow, sides, strip_sides, par, coef, xhi, xlo = prepare(
        x0, params, couple_weight
    )
    strips, low_rows, high_rows = join(strips, west, east, low_rows, high_rows)
    below = lax.ppermute(high_rows, "lat", ring(lat, 1, True))
    above = lax.ppermute(low_rows, "lat", ring(lat, -1, True))
    x0, _, _, *frames, sums, middle = inner(
        strips, x0, xhi, xlo, par, coef, weights, narrow, sides, strip_sides
    )
    new_state, mean, edges, *_ = outer(
        below, above, strips, params, sums, middle, narrow, sides, strip_sides, x0, *frames
    )
    received = lax.ppermute(mean, "comp", [(0, 1), (1, 0)])

    def across(step):
        return [(a * 2 + s, b * 2 + 1 - s) for a, b in ring(lon, step, True) for s in range(2)]

    west_edges = lax.ppermute(edges, ("lon", "comp"), across(1))
    east_edges = lax.ppermute(edges, ("lon", "comp"), across(-1))
    coupled = pl.pallas_call(
        remap_kernel,
        out_shape=jax.ShapeDtypeStruct((1, NQ, ROWS, COLS), F32),
        in_specs=[SMEM] + [VMEM] * 5,
        out_specs=VMEM,
        compiler_params=params_of(16),
        name="remap",
    )(weight_table, received, west_edges, east_edges, intersection_map, sea_mask)
    return new_state, coupled


def solution(mesh):
    placed = (
        P("comp", None, None, "lat", "lon"),
        P("comp", None, None, "lat", "lon"),
        P("comp", None, None, None),
        P("comp", None, None),
        P("comp", "lat", "lon"),
        P("comp", "lat", "lon"),
    )
    return jax.shard_map(
        local,
        mesh=mesh,
        in_specs=placed,
        out_specs=(P("comp", None, None, "lat", "lon"), P("comp", None, "lat", "lon")),
        check_vma=False,
    )
```
